256 devices in a mesh: dp: 2 (over core), ctx: 4 (over x), expert: 32 (over z, y).
Axes of the slice: x: 4, y: 4, z: 8, core: 2. Of those that a mesh axis runs over, the one named last changes fastest.
Arguments:
- tokens: bfloat16 [2, 16384, 2048], P('dp', ('ctx', 'expert')), may hold values from -6 to 6
- out_grad: bfloat16 [2, 16384, 2048], P('dp', ('ctx', 'expert')), may hold values from -6 to 6
- w_in: bfloat16 [32, 2048, 512], P('expert'), may hold values from -0.125 to 0.125
- w_out: bfloat16 [32, 512, 2048], P('expert'), may hold values from -0.25 to 0.25
- picks: int32 [2, 32, 1024], P('dp'), may hold values from 0 to 16383, as said below
- gates: float32 [2, 32, 1024], P('dp', 'expert', 'ctx'), may hold values from 0.1 to 1
Outputs:
- tok_grad: bfloat16 [2, 16384, 2048], P('dp', ('ctx', 'expert'))
- w_in_grad: bfloat16 [32, 2048, 512], P('expert')
- w_out_grad: bfloat16 [32, 512, 2048], P('expert')
- gate_grad: float32 [2, 32, 1024], P('dp', 'expert', 'ctx')
The draws below stay inside these ranges and needn't reach their ends.
Inputs may be any that keep to these rules, and one draw needn't show every extreme that they name: `picks`: for every group and expert the 1024 entries are distinct. Within each quarter of an expert's list (entries q * 256 to (q + 1) * 256 - 1) at most 4 entries fall into any one block of 128 consecutive tokens, and some block holds exactly 4.
All inputs are finite; a program needn't handle non-finite values.
Results may differ from the reference program's by a relative error of at most 0.017.
Values may be sent and summed in bfloat16 or wider, within the bound.
No kernel may reach another device: no remote copies, remote signals or barrier semaphores. Data moves between devices by JAX's collectives and lax.ppermute only.
A program may use at most 128 MiB of HBM per device.

```python
import jax
import jax.numpy as jnp
from jax import lax

D = 2048
EXPERT_HID = 512
TOK_DEV = 128
GROUPS = 2
BLOCKS = 128
GROUP_TOK = 16384
EXPERTS = 32
PICKS = 1024
SHARE = 256
LOAD_MEAN = 2
LOAD_MOST = 4
N_CTX = 4


def one_expert(key):
    quarters = PICKS // SHARE
    key_order, key_shift, key_rows, key_mix = jax.random.split(key, 4)
    orders = jax.vmap(lambda sub_key: jax.random.permutation(sub_key, BLOCKS))(jax.random.split(key_order, quarters))
    shifts = jax.random.randint(key_shift, (quarters, BLOCKS // 2), 0, LOAD_MEAN + 1)
    shifts = shifts.at[:, 0].set(LOAD_MEAN)
    signed = jnp.concatenate([shifts, -shifts], axis=1) + LOAD_MEAN
    counts = jnp.zeros((quarters, BLOCKS), jnp.int32).at[jnp.arange(quarters)[:, None], orders].set(signed.astype(jnp.int32))
    starts = jnp.cumsum(counts, axis=0) - counts
    shuffles = jax.vmap(lambda sub_key: jax.random.permutation(sub_key, TOK_DEV))(jax.random.split(key_rows, BLOCKS))
    offsets = jnp.arange(LOAD_MOST)
    spots = jnp.minimum(starts[:, :, None] + offsets[None, None, :], TOK_DEV - 1)
    block_ids = jnp.arange(BLOCKS)[None, :, None]
    rows_local = shuffles[block_ids, spots]
    token_ids = rows_local + block_ids * TOK_DEV
    live = (offsets[None, None, :] < counts[:, :, None]).astype(jnp.int32)
    flat_ids = token_ids.reshape(quarters, BLOCKS * LOAD_MOST)
    flat_live = live.reshape(quarters, BLOCKS * LOAD_MOST)
    ranking = jnp.argsort(1 - flat_live, axis=1, stable=True)[:, :SHARE]
    taken = jnp.take_along_axis(flat_ids, ranking, axis=1)
    mixes = jax.vmap(lambda sub_key: jax.random.permutation(sub_key, SHARE))(jax.random.split(key_mix, quarters))
    return jnp.take_along_axis(taken, mixes, axis=1).reshape(PICKS)


def draw_picks(key, part):
    key = jax.random.fold_in(key, 7)
    keys = jax.random.split(key, GROUPS * EXPERTS)
    return jax.vmap(one_expert)(keys).reshape(GROUPS, EXPERTS, PICKS).astype(jnp.int32)


def steps_of(key, dims, shards, least, largest):
    gain = 1.0
    for position, parts in shards:
        heights = jax.random.uniform(jax.random.fold_in(jax.random.fold_in(key, 6), position), (parts,), jnp.float32, least / len(shards), largest / len(shards))
        gain = gain * jnp.repeat(jnp.exp(heights), dims[position] // parts).reshape((-1,) + (1,) * (len(dims) - 1 - position))
    return gain


def normal_values(rng, dims, scale, bound, cuts=(), held_as=jnp.bfloat16):
    drawn = scale * jax.random.normal(rng, dims, jnp.float32)
    if cuts:
        drawn = drawn * steps_of(rng, dims, cuts, -0.22, 0.18)
    return jnp.clip(drawn, -bound, bound).astype(held_as)


def setup_inputs(seed: int = 0) -> dict:
    key_list = jax.random.split(jax.random.key(seed), 7)
    tokens = normal_values(key_list[0], (GROUPS, GROUP_TOK, D), 1.0, 6.0, ((0, 2), (1, 128)))
    out_grad = normal_values(key_list[1], (GROUPS, GROUP_TOK, D), 1.0, 6.0, ((0, 2), (1, 128)))
    w_in = normal_values(key_list[2], (EXPERTS, D, EXPERT_HID), D ** -0.5, 0.125, ((0, 32),))
    w_out = normal_values(key_list[3], (EXPERTS, EXPERT_HID, D), EXPERT_HID ** -0.5, 0.25, ((0, 32),))
    picks = draw_picks(jax.random.fold_in(key_list[6], 71), 0)
    gates = jnp.clip(0.1 + 0.9 * jax.random.uniform(key_list[5], (GROUPS, EXPERTS, PICKS), jnp.float32) ** steps_of(key_list[5], (GROUPS, EXPERTS, PICKS), ((0, 2), (1, 32), (2, 4)), -0.2, 0.2), 0.1, 1.0)
    return {"tokens": tokens, "out_grad": out_grad, "w_in": w_in, "w_out": w_out, "picks": picks, "gates": gates}


def silu_slope(pre_act):
    sigmoid_v = jax.nn.sigmoid(pre_act)
    return sigmoid_v * (1.0 + pre_act * (1.0 - sigmoid_v))


def expert_pass(rows_in, rows_grad, gate_rows, weight_in, weight_out):
    pre_act = jnp.dot(rows_in, weight_in, preferred_element_type=jnp.float32)
    activation = jax.nn.silu(pre_act).astype(jnp.bfloat16)
    expert_out = jnp.dot(activation, weight_out, preferred_element_type=jnp.float32)
    gate_part = jnp.sum(rows_grad.astype(jnp.float32) * expert_out, axis=-1)
    scaled = (gate_rows[:, None] * rows_grad.astype(jnp.float32)).astype(jnp.bfloat16)
    act_grad = lax.dot_general(scaled, weight_out, (((1,), (1,)), ((), ())), preferred_element_type=jnp.float32)
    pre_grad = (act_grad * silu_slope(pre_act)).astype(jnp.bfloat16)
    row_grads = lax.dot_general(pre_grad, weight_in, (((1,), (1,)), ((), ())), preferred_element_type=jnp.float32).astype(jnp.bfloat16)
    return activation, scaled, pre_grad, row_grads, gate_part


def reference(tokens, out_grad, w_in, w_out, picks, gates):
    grad_scale = (GROUPS * PICKS) ** -0.5

    def per_expert(token_sum, expert):
        weight_in = w_in[expert]
        weight_out = w_out[expert]
        sum_in = jnp.zeros((D, EXPERT_HID), jnp.float32)
        sum_out = jnp.zeros((EXPERT_HID, D), jnp.float32)
        gate_list = []
        for group_id in range(GROUPS):
            chosen_rows = picks[group_id, expert]
            rows_in = tokens[group_id][chosen_rows]
            rows_grad = out_grad[group_id][chosen_rows]
            activation, scaled, pre_grad, row_grads, gate_part = expert_pass(rows_in, rows_grad, gates[group_id, expert], weight_in, weight_out)
            quart_in = rows_in.astype(jnp.float32).reshape(N_CTX, SHARE, D)
            quart_pre = pre_grad.astype(jnp.float32).reshape(N_CTX, SHARE, EXPERT_HID)
            quart_act = activation.astype(jnp.float32).reshape(N_CTX, SHARE, EXPERT_HID)
            quart_scaled = scaled.astype(jnp.float32).reshape(N_CTX, SHARE, D)
            part_in = jnp.einsum("qsd,qsh->qdh", quart_in, quart_pre, precision=lax.Precision.HIGHEST) * grad_scale
            part_out = jnp.einsum("qsh,qsd->qhd", quart_act, quart_scaled, precision=lax.Precision.HIGHEST) * grad_scale
            sum_in = sum_in + jnp.sum(lax.optimization_barrier(part_in.astype(jnp.bfloat16)).astype(jnp.float32), axis=0)
            sum_out = sum_out + jnp.sum(lax.optimization_barrier(part_out.astype(jnp.bfloat16)).astype(jnp.float32), axis=0)
            token_sum = token_sum.at[group_id, chosen_rows].add(row_grads.astype(jnp.float32))
            gate_list.append(gate_part)
        return token_sum, (sum_in.astype(jnp.bfloat16), sum_out.astype(jnp.bfloat16), jnp.stack(gate_list))

    start_sum = jnp.zeros((GROUPS, GROUP_TOK, D), jnp.float32)
    token_sum, (w_in_grad, w_out_grad, gate_all) = lax.scan(per_expert, start_sum, jnp.arange(EXPERTS, dtype=jnp.int32))
    return token_sum.astype(jnp.bfloat16), w_in_grad, w_out_grad, jnp.transpose(gate_all, (1, 0, 2))
```

```python
import jax
import jax.numpy as jnp
from jax import lax
from jax.sharding import PartitionSpec as P

BF = jnp.bfloat16
F32 = jnp.float32


def dot(left, right, dims):
    return lax.dot_general(left, right, (dims, ((), ())), preferred_element_type=F32)


def ring(count, step):
    return [(i, (i + step) % count) for i in range(count)]


def earlier(count):
    rows = lax.broadcasted_iota(jnp.int32, (count, count), 0)
    cols = lax.broadcasted_iota(jnp.int32, (count, count), 1)
    return (rows < cols).astype(BF)


def reduce_dp(part):
    core = lax.axis_index("dp")
    half = part.shape[0] // 2
    mine = lax.dynamic_slice_in_dim(part, core * half, half)
    other = lax.dynamic_slice_in_dim(part, (1 - core) * half, half)
    got = lax.ppermute(other, "dp", ring(2, 1))
    return (mine.astype(F32) + got.astype(F32)).astype(BF)


def gather_dp(part):
    core = lax.axis_index("dp")
    other = lax.ppermute(part, "dp", ring(2, 1))
    return jnp.where(
        core == 0, jnp.concatenate((part, other), 0), jnp.concatenate((other, part), 0)
    )


def reduce_ctx(part):
    count = lax.axis_size("ctx")
    index = lax.axis_index("ctx")
    size = part.shape[0] // count

    def piece(step):
        return lax.dynamic_slice_in_dim(part, ((index + step) % count) * size, size)

    steps = (2, 1, 3)
    got = [lax.ppermute(piece(step), "ctx", ring(count, step)) for step in steps]
    total = piece(0).astype(F32)
    for term in got:
        total = total + term.astype(F32)
    total = total.astype(BF)
    whole = jnp.zeros_like(part)
    whole = lax.dynamic_update_slice_in_dim(whole, total, index * size, 0)
    for step in steps:
        term = lax.ppermute(total, "ctx", ring(count, step))
        whole = lax.dynamic_update_slice_in_dim(whole, term, ((index - step) % count) * size, 0)
    return whole


def shards(tokens, out_grad, w_in, w_out, picks, gates):
    ctx_count = lax.axis_size("ctx")
    exp_count = lax.axis_size("expert")
    ctx_index = lax.axis_index("ctx")
    exp_index = lax.axis_index("expert")
    tok_dev, feat = tokens.shape[1], tokens.shape[2]
    pick_total = picks.shape[2]
    share = pick_total // ctx_count
    slots = ctx_count * 4
    slot_rows = exp_count * slots
    grad_scale = (lax.axis_size("dp") * pick_total) ** (-0.5)
    lists = picks[0]
    before = earlier(tok_dev)
    tok_ids = jnp.arange(tok_dev, dtype=jnp.int32)
    slot_ids = jnp.arange(slots, dtype=jnp.int32)

    local = lists - (ctx_index * exp_count + exp_index) * tok_dev
    picked = jnp.any(local[:, :, None] == tok_ids[None, None, :], axis=1)
    rank = dot(picked.astype(BF), before, ((1,), (0,))).astype(jnp.int32)
    spread = picked[:, None, :] & (rank[:, None, :] == slot_ids[None, :, None])
    spread = spread.astype(BF).reshape(slot_rows, tok_dev)

    def send(rows):
        out = dot(spread, rows, ((1,), (0,))).astype(BF)
        out = lax.all_to_all(
            out.reshape(exp_count, slots, feat), "expert", split_axis=0, concat_axis=0, tiled=True
        )
        return out.reshape(slot_rows, feat)

    rows_in = send(tokens[0])
    rows_grad = send(out_grad[0])

    own = lax.dynamic_index_in_dim(lists, exp_index, 0, keepdims=False)
    offset = own - ctx_index * (exp_count * tok_dev)
    block = offset // tok_dev
    inside = (block >= 0) & (block < exp_count)
    token = offset % tok_dev
    in_block = (inside[:, None] & (block[:, None] == jnp.arange(exp_count)[None, :])).astype(BF)
    at_token = (token[:, None] == tok_ids[None, :]).astype(BF)
    held = dot(in_block, at_token, ((0,), (0,))).astype(BF)
    rank_own = dot(held, before, ((1,), (0,))).astype(BF)
    rank_pick = jnp.sum(
        dot(in_block, rank_own, ((1,), (0,))) * at_token.astype(F32), axis=1
    ).astype(jnp.int32)
    place = jnp.where(inside, block * slots + rank_pick, -1)
    at_slot = place[:, None] == jnp.arange(slot_rows, dtype=jnp.int32)[None, :]
    gate_all = lax.all_gather(gates[0, 0], "ctx", tiled=True)
    slot_gate = jnp.sum(jnp.where(at_slot, gate_all[:, None], 0.0), axis=0)

    weight_in = w_in[0]
    weight_out = w_out[0]
    pre_act = dot(rows_in, weight_in, ((1,), (0,)))
    sig = jax.nn.sigmoid(pre_act)
    activation = (pre_act * sig).astype(BF)
    slope = sig * (1.0 + pre_act * (1.0 - sig))
    back = dot(rows_grad, weight_out, ((1,), (1,)))
    pre_grad = (slot_gate[:, None] * back * slope).astype(BF)
    row_grads = dot(pre_grad, weight_in, ((1,), (1,))).astype(BF)
    returned = lax.all_to_all(
        row_grads.reshape(exp_count, slots, feat), "expert", split_axis=0, concat_axis=0, tiled=True
    ).reshape(slot_rows, feat)

    gated = (slot_gate[:, None] * activation.astype(F32)).astype(BF)
    out_part = (dot(gated, rows_grad, ((0,), (0,))) * grad_scale).astype(BF)
    in_part = (dot(rows_in, pre_grad, ((0,), (0,))) * grad_scale).astype(BF)
    out_total = gather_dp(reduce_ctx(reduce_dp(out_part)))
    in_total = gather_dp(reduce_ctx(reduce_dp(in_part)))

    gate_slot = jnp.sum(activation.astype(F32) * back, axis=1)
    gate_pick = jnp.sum(jnp.where(at_slot, gate_slot[None, :], 0.0), axis=1)
    gate_grad = lax.psum_scatter(gate_pick, "ctx", tiled=True)

    token_total = dot(spread, returned, ((0,), (0,))).astype(BF)
    return (
        token_total[None],
        in_total[None],
        out_total[None],
        gate_grad.reshape(1, 1, share),
    )


def solution(mesh):
    placed = (
        P("dp", ("ctx", "expert"), None),
        P("dp", ("ctx", "expert"), None),
        P("expert", None, None),
        P("expert", None, None),
        P("dp", None, None),
        P("dp", "expert", "ctx"),
    )
    return jax.shard_map(
        shards,
        mesh=mesh,
        in_specs=placed,
        out_specs=(
            P("dp", ("ctx", "expert"), None),
            P("expert", None, None),
            P("expert", None, None),
            P("dp", "expert", "ctx"),
        ),
        check_vma=False,
    )
```

```python
import jax
import jax.numpy as jnp
from jax import lax
from jax.experimental import pallas as pl
from jax.experimental.pallas import tpu as pltpu
from jax.sharding import PartitionSpec as P

BF = jnp.bfloat16
F32 = jnp.float32
I32 = jnp.int32
NEAR = ((0, 1), (1, 0), (2, 3), (3, 2))
FAR = ((0, 3), (3, 0), (1, 2), (2, 1))
SWAP = ((0, 1), (1, 0))


def dot(left, right, dims):
    return lax.dot_general(left, right, (dims, ((), ())), preferred_element_type=F32)


def ring(count, step):
    return [(i, (i + step) % count) for i in range(count)]


def earlier(count):
    rows = lax.broadcasted_iota(I32, (count, count), 0)
    cols = lax.broadcasted_iota(I32, (count, count), 1)
    return (rows < cols).astype(BF)


def bits(ctx_index):
    high = ctx_index // 2
    return (ctx_index % 2 + high) % 2, high


def halve(part, keep, pairs):
    size = part.shape[0] // 2
    sent = lax.ppermute(lax.dynamic_slice_in_dim(part, (1 - keep) * size, size), "ctx", pairs)
    mine = lax.dynamic_slice_in_dim(part, keep * size, size)
    return (mine.astype(F32) + sent.astype(F32)).astype(BF)


def reduce_ctx(part, first, second):
    (keep_a, pairs_a), (keep_b, pairs_b) = first, second
    piece = halve(halve(part, keep_a, pairs_a), keep_b, pairs_b)
    side = lax.ppermute(piece, "ctx", pairs_b)
    across = lax.ppermute(piece, "ctx", pairs_a)
    corner = lax.ppermute(side, "ctx", pairs_a)
    own = (piece, side, across, corner)
    return own + tuple(lax.ppermute(term, "dp", SWAP) for term in own)


def assemble_kernel(where, *refs):
    out_pieces, in_pieces = refs[:8], refs[8:16]
    out_ref, in_ref, sems = refs[16], refs[17], refs[18]
    core, near, far = where[0], where[1], where[2]
    out_rows, in_rows, in_cols = out_pieces[0].shape[0], in_pieces[0].shape[0], in_pieces[0].shape[1]
    copies = []
    for k in range(8):
        half = core if k < 4 else 1 - core
        flip_b, flip_a = k % 2, (k // 2) % 2
        a = 1 - near if flip_a else near
        b = 1 - far if flip_b else far
        row = pl.multiple_of(((half * 2 + a) * 2 + b) * out_rows, out_rows)
        copies.append(
            pltpu.make_async_copy(out_pieces[k], out_ref.at[pl.ds(row, out_rows), :], sems.at[k])
        )
        a = 1 - far if flip_a else far
        b = 1 - near if flip_b else near
        row = pl.multiple_of((a * 2 + b) * in_rows, in_rows)
        col = pl.multiple_of(half * in_cols, in_cols)
        copies.append(
            pltpu.make_async_copy(
                in_pieces[k],
                in_ref.at[pl.ds(row, in_rows), pl.ds(col, in_cols)],
                sems.at[8 + k],
            )
        )
    for copy in copies:
        copy.start()
    for copy in copies:
        copy.wait()


def assemble(where, out_pieces, in_pieces, out_shape, in_shape):
    moved = 4 * (out_shape[0] * out_shape[1] + in_shape[0] * in_shape[1])
    return pl.pallas_call(
        assemble_kernel,
        in_specs=[pl.BlockSpec(memory_space=pltpu.SMEM)]
        + [pl.BlockSpec(memory_space=pl.ANY)] * 16,
        out_specs=[pl.BlockSpec(memory_space=pl.ANY)] * 2,
        out_shape=[jax.ShapeDtypeStruct(out_shape, BF), jax.ShapeDtypeStruct(in_shape, BF)],
        scratch_shapes=[pltpu.SemaphoreType.DMA((16,))],
        cost_estimate=pl.CostEstimate(flops=0, bytes_accessed=moved, transcendentals=0),
    )(where, *out_pieces, *in_pieces)


def shards(tokens, out_grad, w_in, w_out, picks, gates):
    ctx_count = lax.axis_size("ctx")
    exp_count = lax.axis_size("expert")
    core = lax.axis_index("dp")
    ctx_index = lax.axis_index("ctx")
    exp_index = lax.axis_index("expert")
    tok_dev, feat = tokens.shape[1], tokens.shape[2]
    hid = w_in.shape[2]
    pick_total = picks.shape[2]
    share = pick_total // ctx_count
    slots = ctx_count * 4
    low = slots // 2
    cuts = ((0, low), (low, slots))
    grad_scale = (lax.axis_size("dp") * pick_total) ** (-0.5)
    lists = picks[0]
    before = earlier(tok_dev)
    tok_ids = jnp.arange(tok_dev, dtype=I32)

    local = lists - (ctx_index * exp_count + exp_index) * tok_dev
    picked = jnp.any(local[:, :, None] == tok_ids[None, None, :], axis=1)
    rank = dot(picked.astype(BF), before, ((1,), (0,))).astype(I32)
    both = jnp.concatenate((tokens[0], out_grad[0]), axis=1)

    def spread_of(cut):
        start, end = cut
        slot_ids = jnp.arange(start, end, dtype=I32)
        spread = picked[:, None, :] & (rank[:, None, :] == slot_ids[None, :, None])
        return spread.astype(BF).reshape(exp_count * (end - start), tok_dev)

    def swap(rows):
        out = rows.reshape(exp_count, -1, rows.shape[1])
        out = lax.all_to_all(out, "expert", split_axis=0, concat_axis=0, tiled=True)
        return out.reshape(rows.shape)

    spreads = [spread_of(cut) for cut in cuts]
    arrived = [swap(dot(spread, both, ((1,), (0,))).astype(BF)) for spread in spreads]

    own = lax.dynamic_index_in_dim(lists, exp_index, 0, keepdims=False)
    offset = own - ctx_index * (exp_count * tok_dev)
    block = offset // tok_dev
    inside = (block >= 0) & (block < exp_count)
    token = offset % tok_dev
    in_block = (inside[:, None] & (block[:, None] == jnp.arange(exp_count)[None, :])).astype(BF)
    at_token = (token[:, None] == tok_ids[None, :]).astype(BF)
    held = dot(in_block, at_token, ((0,), (0,))).astype(BF)
    rank_own = dot(held, before, ((1,), (0,))).astype(BF)
    rank_pick = jnp.sum(
        dot(in_block, rank_own, ((1,), (0,))) * at_token.astype(F32), axis=1
    ).astype(I32)
    gate_mine = gates[0, 0]
    gate_all = jnp.zeros((ctx_count, share), F32)
    gate_all = lax.dynamic_update_slice_in_dim(gate_all, gate_mine[None], ctx_index, 0)
    for step in range(1, ctx_count):
        got = lax.ppermute(gate_mine, "ctx", ring(ctx_count, step))
        gate_all = lax.dynamic_update_slice_in_dim(
            gate_all, got[None], (ctx_index - step) % ctx_count, 0
        )
    gate_all = gate_all.reshape(pick_total)

    weight_in = w_in[0]
    weight_out = w_out[0]
    other = (1 - core) * (hid // 2)
    mine = core * (hid // 2)
    sums = {"out_other": 0.0, "out_mine": 0.0, "in_other": 0.0, "in_mine": 0.0}
    gate_pick = jnp.zeros((pick_total,), F32)
    returned = []
    for (start, end), rows in zip(cuts, arrived):
        width = end - start
        rows_in, rows_grad = rows[:, :feat], rows[:, feat:]
        fits = inside & (rank_pick >= start) & (rank_pick < end)
        place = jnp.where(fits, block * width + rank_pick - start, -1)
        at_slot = place[:, None] == jnp.arange(exp_count * width, dtype=I32)[None, :]
        slot_gate = jnp.sum(jnp.where(at_slot, gate_all[:, None], 0.0), axis=0)[:, None]
        pre_act = dot(rows_in, weight_in, ((1,), (0,)))
        sig = jax.nn.sigmoid(pre_act)
        activation = (pre_act * sig).astype(BF)
        slope = sig * (1.0 + pre_act * (1.0 - sig))
        back = dot(rows_grad, weight_out, ((1,), (1,)))
        pre_grad = (slot_gate * back * slope).astype(BF)
        gated = (slot_gate * activation.astype(F32)).astype(BF)
        row_grads = dot(pre_grad, weight_in, ((1,), (1,))).astype(BF)
        returned.append(swap(row_grads))
        gate_slot = jnp.sum(activation.astype(F32) * back, axis=1)
        gate_pick += jnp.sum(jnp.where(at_slot, gate_slot[None, :], 0.0), axis=1)
        for name, at in (("other", other), ("mine", mine)):
            cols = lax.dynamic_slice_in_dim(gated, at, hid // 2, 1)
            sums["out_" + name] += dot(cols, rows_grad, ((0,), (0,)))
            cols = lax.dynamic_slice_in_dim(pre_grad, at, hid // 2, 1)
            sums["in_" + name] += dot(rows_in, cols, ((0,), (0,)))

    near, far = bits(ctx_index)
    pieces = []
    for name, order in (
        ("out_", ((near, NEAR), (far, FAR))),
        ("in_", ((far, FAR), (near, NEAR))),
    ):
        sent = lax.ppermute((sums[name + "other"] * grad_scale).astype(BF), "dp", SWAP)
        half = (sums[name + "mine"] * grad_scale + sent.astype(F32)).astype(BF)
        pieces.append(reduce_ctx(half, *order))
    out_total, in_total = assemble(
        jnp.stack((core, near, far)).astype(I32), *pieces, (hid, feat), (feat, hid)
    )

    gate_rows = gate_pick.reshape(ctx_count, share)
    gate_grad = lax.dynamic_index_in_dim(gate_rows, ctx_index, 0, keepdims=False)
    for step in range(1, ctx_count):
        term = lax.dynamic_index_in_dim(
            gate_rows, (ctx_index + step) % ctx_count, 0, keepdims=False
        )
        gate_grad = gate_grad + lax.ppermute(term, "ctx", ring(ctx_count, step))

    token_total = sum(dot(spread, rows, ((0,), (0,))) for spread, rows in zip(spreads, returned))
    return (
        token_total.astype(BF)[None],
        in_total[None],
        out_total[None],
        gate_grad.reshape(1, 1, share),
    )


def solution(mesh):
    placed = (
        P("dp", ("ctx", "expert"), None),
        P("dp", ("ctx", "expert"), None),
        P("expert", None, None),
        P("expert", None, None),
        P("dp", None, None),
        P("dp", "expert", "ctx"),
    )
    return jax.shard_map(
        shards,
        mesh=mesh,
        in_specs=placed,
        out_specs=(
            P("dp", ("ctx", "expert"), None),
            P("expert", None, None),
            P("expert", None, None),
            P("dp", "expert", "ctx"),
        ),
        check_vma=False,
    )
```

```python
import functools

import jax
import jax.numpy as jnp
from jax import lax
from jax.experimental import pallas as pl
from jax.experimental.pallas import tpu as pltpu
from jax.sharding import PartitionSpec as P

BF = jnp.bfloat16
F32 = jnp.float32
I32 = jnp.int32
SWAP = ((0, 1), (1, 0))
NEAR = ((0, 1), (1, 0), (2, 3), (3, 2))
FAR = ((0, 3), (3, 0), (1, 2), (2, 1))


def dot(left, right, dims):
    return lax.dot_general(left, right, (dims, ((), ())), preferred_element_type=F32)


def ring(count, step):
    return [(i, (i + step) % count) for i in range(count)]


def earlier(count):
    rows = lax.broadcasted_iota(I32, (count, count), 0)
    cols = lax.broadcasted_iota(I32, (count, count), 1)
    return (rows < cols).astype(BF)


def bits(ctx_index):
    high = ctx_index // 2
    return (ctx_index % 2 + high) % 2, high


def reduce_ctx(parts, near, far, beside):
    join = lax.optimization_barrier
    plans = (((near, NEAR), (far, FAR)), ((far, FAR), (near, NEAR)))
    for step in range(2):
        sent, kept = [], []
        for part, plan in zip(parts, plans):
            keep = plan[step][0]
            size = part.shape[0] // 2
            sent.append(lax.dynamic_slice_in_dim(part, (1 - keep) * size, size))
            kept.append(lax.dynamic_slice_in_dim(part, keep * size, size))
        sent, kept = join((sent, kept))
        got = [lax.ppermute(part, "ctx", plan[step][1]) for part, plan in zip(sent, plans)]
        got, kept, beside = join((got, kept, beside))
        parts = [(a.astype(F32) + b.astype(F32)).astype(BF) for a, b in zip(kept, got)]
    parts = join(parts)
    side = [lax.ppermute(part, "ctx", plan[1][1]) for part, plan in zip(parts, plans)]
    across = [lax.ppermute(part, "ctx", plan[0][1]) for part, plan in zip(parts, plans)]
    side = join(side)
    corner = [lax.ppermute(part, "ctx", plan[0][1]) for part, plan in zip(side, plans)]
    return [tuple(four) for four in zip(parts, side, across, corner)], beside


def dispatch_kernel(base, picks, tokens, out_grad, sent, spread, high_ref, low_ref, code_ref):
    exp_count, tok_dev = code_ref.shape
    highs, lows = high_ref.shape[0] // exp_count, low_ref.shape[0] // exp_count
    rows = spread.shape[0]
    slots = rows * pl.num_programs(0) // exp_count
    iota = lax.broadcasted_iota

    @pl.when(pl.program_id(0) == 0)
    def _():
        for e in range(exp_count):
            local = picks[0, e : e + 1, :] - base[0]
            wide = (highs, local.shape[1])
            high_ref[e * highs : (e + 1) * highs, :] = (
                iota(I32, wide, 0) == jnp.broadcast_to(local >> (lows.bit_length() - 1), wide)
            ).astype(F32)
            wide = (lows, local.shape[1])
            low_ref[e * lows : (e + 1) * lows, :] = (
                iota(I32, wide, 0) == jnp.broadcast_to(local & (lows - 1), wide)
            ).astype(F32)
        pairs = dot(high_ref[...].astype(BF), low_ref[...].astype(BF), ((1,), (1,)))
        same = iota(I32, pairs.shape, 0) // highs == iota(I32, pairs.shape, 1) // lows
        pairs = jnp.where(same, pairs, 0.0).astype(BF)
        wide = (exp_count * lows, tok_dev)
        fold = (iota(I32, wide, 0) % lows == iota(I32, wide, 1) % lows).astype(BF)
        by_high = dot(pairs, fold, ((1,), (0,)))
        same = iota(I32, by_high.shape, 0) % highs == iota(I32, by_high.shape, 1) // lows
        by_high = jnp.where(same, by_high, 0.0).astype(BF)
        wide = (exp_count, exp_count * highs)
        fold = (iota(I32, wide, 0) == iota(I32, wide, 1) // highs).astype(BF)
        picked = dot(fold, by_high, ((1,), (0,)))
        rank = dot(picked.astype(BF), earlier(tok_dev), ((1,), (0,)))
        code_ref[...] = picked * (rank + 1.0)

    wide = (rows, exp_count)
    at = pl.program_id(0) * (rows // slots)
    repeat = (iota(I32, wide, 0) // slots + at == iota(I32, wide, 1)).astype(BF)
    code = dot(repeat, code_ref[...].astype(BF), ((1,), (0,)))
    slot = (iota(I32, code.shape, 0) % slots + 1).astype(F32)
    chosen = (code == slot).astype(F32).astype(BF)
    spread[...] = chosen
    feat = tokens.shape[2]
    sent[:, :feat] = dot(chosen, tokens[0], ((1,), (0,))).astype(BF)
    sent[:, feat:] = dot(chosen, out_grad[0], ((1,), (0,))).astype(BF)


def dispatch(base, picks, tokens, out_grad, slots):
    exp_count, pick_total = picks.shape[1:]
    tok_dev, feat = tokens.shape[1:]
    lows = 16
    steps = 4
    rows = exp_count * slots // steps

    def whole(shape):
        return pl.BlockSpec(shape, lambda i: (0,) * len(shape))

    return pl.pallas_call(
        dispatch_kernel,
        grid=(steps,),
        in_specs=[
            pl.BlockSpec(memory_space=pltpu.SMEM),
            whole(picks.shape),
            whole(tokens.shape),
            whole(out_grad.shape),
        ],
        out_specs=[
            pl.BlockSpec((rows, 2 * feat), lambda i: (i, 0)),
            pl.BlockSpec((rows, tok_dev), lambda i: (i, 0)),
        ],
        out_shape=[
            jax.ShapeDtypeStruct((exp_count * slots, 2 * feat), BF),
            jax.ShapeDtypeStruct((exp_count * slots, tok_dev), BF),
        ],
        scratch_shapes=[
            pltpu.VMEM((exp_count * tok_dev // lows, pick_total), F32),
            pltpu.VMEM((exp_count * lows, pick_total), F32),
            pltpu.VMEM((exp_count, tok_dev), F32),
        ],
        compiler_params=pltpu.CompilerParams(vmem_limit_bytes=32 * 1024 * 1024),
        cost_estimate=pl.CostEstimate(
            flops=4 * exp_count * slots * tok_dev * feat,
            bytes_accessed=4 * exp_count * slots * feat,
            transcendentals=0,
        ),
    )(jnp.reshape(base, (1,)).astype(I32), picks, tokens, out_grad)


def pass_kernel(rows_in, rows_grad, weight_in, weight_out, gate, grads, pre, gated, gate_slot):
    pre_act = dot(rows_in[...], weight_in[...], ((1,), (0,)))
    back = dot(rows_grad[...], weight_out[...], ((1,), (1,)))
    sig = 1.0 / (1.0 + jnp.exp(-pre_act))
    activation = (pre_act * sig).astype(BF).astype(F32)
    pre_grad = (gate[...] * back * (sig * (1.0 + pre_act * (1.0 - sig)))).astype(BF)
    gate_slot[...] = jnp.sum(activation * back, axis=1, keepdims=True)
    gated[...] = (gate[...] * activation).astype(BF)
    pre[...] = pre_grad
    grads[...] = dot(pre_grad, weight_in[...], ((1,), (1,))).astype(BF)


def expert_pass(rows, weight_in, weight_out, gate):
    count, feat, hid = rows.shape[0], weight_in.shape[0], weight_in.shape[1]
    size = min(256, count)

    def block(cols, at=0):
        return pl.BlockSpec((size, cols), lambda i: (i, at))

    def whole(shape):
        return pl.BlockSpec(shape, lambda i: (0, 0))

    return pl.pallas_call(
        pass_kernel,
        grid=(count // size,),
        in_specs=[
            block(feat),
            block(feat, 1),
            whole((feat, hid)),
            whole((hid, feat)),
            block(1),
        ],
        out_specs=[block(feat), block(hid), block(hid), block(1)],
        out_shape=[
            jax.ShapeDtypeStruct((count, feat), BF),
            jax.ShapeDtypeStruct((count, hid), BF),
            jax.ShapeDtypeStruct((count, hid), BF),
            jax.ShapeDtypeStruct((count, 1), F32),
        ],
        compiler_params=pltpu.CompilerParams(vmem_limit_bytes=48 * 1024 * 1024),
        cost_estimate=pl.CostEstimate(
            flops=6 * count * feat * hid,
            bytes_accessed=2 * (3 * count * feat + 2 * feat * hid),
            transcendentals=count * hid,
        ),
    )(rows, rows, weight_in, weight_out, gate)


def outer_kernel(scale, where, rows_in, rows_grad, pre_a, pre_b, gated_a, gated_b, *refs):
    half = pre_a.shape[1]
    gated = jnp.concatenate((gated_a[...], gated_b[...]), axis=1)
    pre = jnp.concatenate((pre_a[...], pre_b[...]), axis=1)
    out = (dot(gated, rows_grad[...], ((0,), (0,))) * scale).astype(BF)
    inn = (dot(rows_in[...], pre, ((0,), (0,))) * scale).astype(BF)
    refs[0][...], refs[2][...] = out[:half], out[half:]
    refs[1][...], refs[3][...] = inn[:, :half], inn[:, half:]


def outer(rows, pre, gated, core, scale):
    count, feat, hid = rows.shape[0], rows.shape[1] // 2, pre.shape[1] // 2
    steps = 4
    size = feat // steps
    out_block = pl.BlockSpec((hid, size), lambda i, at: (0, i))
    in_block = pl.BlockSpec((size, hid), lambda i, at: (i, 0))
    theirs = pl.BlockSpec((count, hid), lambda i, at: (0, 1 - at[0]))
    mine = pl.BlockSpec((count, hid), lambda i, at: (0, at[0]))
    out_type = jax.ShapeDtypeStruct((hid, feat), BF)
    in_type = jax.ShapeDtypeStruct((feat, hid), BF)
    parts = pl.pallas_call(
        functools.partial(outer_kernel, scale),
        grid_spec=pltpu.PrefetchScalarGridSpec(
            num_scalar_prefetch=1,
            grid=(steps,),
            in_specs=[
                pl.BlockSpec((count, size), lambda i, at: (0, i)),
                pl.BlockSpec((count, size), lambda i, at: (0, i + steps)),
                theirs,
                mine,
                theirs,
                mine,
            ],
            out_specs=[out_block, in_block] * 2,
        ),
        out_shape=[out_type, in_type] * 2,
        compiler_params=pltpu.CompilerParams(vmem_limit_bytes=48 * 1024 * 1024),
        cost_estimate=pl.CostEstimate(
            flops=8 * count * feat * hid,
            bytes_accessed=4 * (count * feat + 2 * feat * hid),
            transcendentals=0,
        ),
    )(jnp.reshape(core, (1,)).astype(I32), rows, rows, pre, pre, gated, gated)
    return parts[:2], parts[2:]


def assemble_kernel(where, *refs):
    out_pieces, in_pieces = refs[:8], refs[8:16]
    out_ref, in_ref = refs[16], refs[17]
    core, near, far = where[0], where[1], where[2]
    out_rows, in_rows, in_cols = out_pieces[0].shape[0], in_pieces[0].shape[0], in_pieces[0].shape[1]
    for k in range(8):
        half = core if k < 4 else 1 - core
        flip_b, flip_a = k % 2, (k // 2) % 2
        a = 1 - near if flip_a else near
        b = 1 - far if flip_b else far
        row = pl.multiple_of(((half * 2 + a) * 2 + b) * out_rows, out_rows)
        out_ref[pl.ds(row, out_rows), :] = out_pieces[k][...]
        a = 1 - far if flip_a else far
        b = 1 - near if flip_b else near
        row = pl.multiple_of((a * 2 + b) * in_rows, in_rows)
        col = pl.multiple_of(half * in_cols, in_cols)
        in_ref[pl.ds(row, in_rows), pl.ds(col, in_cols)] = in_pieces[k][...]


def assemble(where, out_pieces, in_pieces, out_shape, in_shape):
    moved = 4 * (out_shape[0] * out_shape[1] + in_shape[0] * in_shape[1])
    return pl.pallas_call(
        assemble_kernel,
        in_specs=[pl.BlockSpec(memory_space=pltpu.SMEM)]
        + [pl.BlockSpec(memory_space=pltpu.VMEM)] * 16,
        out_specs=[pl.BlockSpec(memory_space=pltpu.VMEM)] * 2,
        out_shape=[jax.ShapeDtypeStruct(out_shape, BF), jax.ShapeDtypeStruct(in_shape, BF)],
        compiler_params=pltpu.CompilerParams(vmem_limit_bytes=24 * 1024 * 1024),
        cost_estimate=pl.CostEstimate(flops=0, bytes_accessed=moved, transcendentals=0),
    )(where, *out_pieces, *in_pieces)


def shards(tokens, out_grad, w_in, w_out, picks, gates):
    ctx_count = lax.axis_size("ctx")
    exp_count = lax.axis_size("expert")
    core = lax.axis_index("dp")
    ctx_index = lax.axis_index("ctx")
    exp_index = lax.axis_index("expert")
    tok_dev, feat = tokens.shape[1], tokens.shape[2]
    hid = w_in.shape[2]
    pick_total = picks.shape[2]
    share = pick_total // ctx_count
    slots = ctx_count * 4
    grad_scale = (lax.axis_size("dp") * pick_total) ** (-0.5)
    lists = picks[0]
    before = earlier(tok_dev)
    tok_ids = jnp.arange(tok_dev, dtype=I32)

    def swap(rows):
        out = rows.reshape(exp_count, -1, rows.shape[1])
        out = lax.all_to_all(out, "expert", split_axis=0, concat_axis=0, tiled=True)
        return out.reshape(rows.shape)

    base = (ctx_index * exp_count + exp_index) * tok_dev
    sent, spread = dispatch(base, picks, tokens, out_grad, slots)
    arrived = swap(sent)

    own = lax.dynamic_index_in_dim(lists, exp_index, 0, keepdims=False)
    offset = own - ctx_index * (exp_count * tok_dev)
    block = offset // tok_dev
    inside = (block >= 0) & (block < exp_count)
    token = offset % tok_dev
    in_block = (inside[:, None] & (block[:, None] == jnp.arange(exp_count)[None, :])).astype(BF)
    at_token = (token[:, None] == tok_ids[None, :]).astype(BF)
    held = dot(in_block, at_token, ((0,), (0,))).astype(BF)
    rank_own = dot(held, before, ((1,), (0,))).astype(BF)
    rank_pick = jnp.sum(
        dot(in_block, rank_own, ((1,), (0,))) * at_token.astype(F32), axis=1
    ).astype(I32)
    gate_mine = gates[0, 0]
    gate_all = jnp.zeros((ctx_count, share), F32)
    gate_all = lax.dynamic_update_slice_in_dim(gate_all, gate_mine[None], ctx_index, 0)
    for step in range(1, ctx_count):
        got = lax.ppermute(gate_mine, "ctx", ring(ctx_count, step))
        gate_all = lax.dynamic_update_slice_in_dim(
            gate_all, got[None], (ctx_index - step) % ctx_count, 0
        )
    gate_all = gate_all.reshape(pick_total)

    place = jnp.where(inside, block * slots + rank_pick, -1)
    at_slot = place[:, None] == jnp.arange(exp_count * slots, dtype=I32)[None, :]
    slot_gate = jnp.sum(jnp.where(at_slot, gate_all[:, None], 0.0), axis=0)[:, None]

    row_grads, pre_grad, gated, gate_slot = expert_pass(arrived, w_in[0], w_out[0], slot_gate)
    theirs, mine = outer(arrived, pre_grad, gated, core, grad_scale)
    got = [lax.ppermute(part, "dp", SWAP) for part in theirs]
    row_grads, _ = lax.optimization_barrier((row_grads, theirs))
    returned = swap(row_grads)
    halves = [(a.astype(F32) + b.astype(F32)).astype(BF) for a, b in zip(mine, got)]

    gate_pick = jnp.sum(jnp.where(at_slot, gate_slot[:, 0][None, :], 0.0), axis=1)
    gate_rows = gate_pick.reshape(ctx_count, share)
    gate_grad = lax.dynamic_index_in_dim(gate_rows, ctx_index, 0, keepdims=False)
    for step in range(1, ctx_count):
        term = lax.dynamic_index_in_dim(
            gate_rows, (ctx_index + step) % ctx_count, 0, keepdims=False
        )
        gate_grad = gate_grad + lax.ppermute(term, "ctx", ring(ctx_count, step))

    near, far = bits(ctx_index)
    pieces, gate_grad = reduce_ctx(halves, near, far, gate_grad)
    pieces = [four + tuple(lax.ppermute(term, "dp", SWAP) for term in four) for four in pieces]
    token_total = dot(spread, returned, ((0,), (0,))).astype(BF)
    pieces, token_total = lax.optimization_barrier((pieces, token_total))
    out_total, in_total = assemble(
        jnp.stack((core, near, far)).astype(I32), *pieces, (hid, feat), (feat, hid)
    )

    return (
        token_total[None],
        in_total[None],
        out_total[None],
        gate_grad.reshape(1, 1, share),
    )


def solution(mesh):
    placed = (
        P("dp", ("ctx", "expert"), None),
        P("dp", ("ctx", "expert"), None),
        P("expert", None, None),
        P("expert", None, None),
        P("dp", None, None),
        P("dp", "expert", "ctx"),
    )
    return jax.shard_map(
        shards,
        mesh=mesh,
        in_specs=placed,
        out_specs=(
            P("dp", ("ctx", "expert"), None),
            P("expert", None, None),
            P("expert", None, None),
            P("dp", "expert", "ctx"),
        ),
        check_vma=False,
    )
```

```python
import functools

import jax
import jax.numpy as jnp
from jax import lax
from jax.experimental import pallas as pl
from jax.experimental.pallas import tpu as pltpu
from jax.sharding import PartitionSpec as P

BF = jnp.bfloat16
F32 = jnp.float32
I32 = jnp.int32
SWAP = ((0, 1), (1, 0))
NEAR = ((0, 1), (1, 0), (2, 3), (3, 2))
FAR = ((0, 3), (3, 0), (1, 2), (2, 1))


def dot(left, right, dims):
    return lax.dot_general(left, right, (dims, ((), ())), preferred_element_type=F32)


def ring(count, step):
    return [(i, (i + step) % count) for i in range(count)]


def earlier(count):
    rows = lax.broadcasted_iota(I32, (count, count), 0)
    cols = lax.broadcasted_iota(I32, (count, count), 1)
    return (rows < cols).astype(BF)


def bits(ctx_index):
    high = ctx_index // 2
    return (ctx_index % 2 + high) % 2, high


def reduce_ctx(parts, near, far, beside):
    join = lax.optimization_barrier
    plans = (((near, NEAR), (far, FAR)), ((far, FAR), (near, NEAR)))
    for step in range(2):
        sent, kept = [], []
        for part, plan in zip(parts, plans):
            keep = plan[step][0]
            size = part.shape[0] // 2
            sent.append(lax.dynamic_slice_in_dim(part, (1 - keep) * size, size))
            kept.append(lax.dynamic_slice_in_dim(part, keep * size, size))
        sent, kept = join((sent, kept))
        got = [lax.ppermute(part, "ctx", plan[step][1]) for part, plan in zip(sent, plans)]
        got, kept, beside = join((got, kept, beside))
        parts = [(a.astype(F32) + b.astype(F32)).astype(BF) for a, b in zip(kept, got)]
    parts = join(parts)
    side = [lax.ppermute(part, "ctx", plan[1][1]) for part, plan in zip(parts, plans)]
    across = [lax.ppermute(part, "ctx", plan[0][1]) for part, plan in zip(parts, plans)]
    side = join(side)
    corner = [lax.ppermute(part, "ctx", plan[0][1]) for part, plan in zip(side, plans)]
    across, corner = join((across, corner))
    return [tuple(four) for four in zip(parts, side, across, corner)], beside


def dispatch_kernel(base, picks, tokens, out_grad, sent, spread, high_ref, low_ref, code_ref):
    exp_count, tok_dev = code_ref.shape
    highs, lows = high_ref.shape[0] // exp_count, low_ref.shape[0] // exp_count
    rows = spread.shape[1]
    slots = rows * pl.num_programs(0) // exp_count
    iota = lax.broadcasted_iota

    @pl.when(pl.program_id(0) == 0)
    def _():
        for e in range(exp_count):
            local = picks[0, e : e + 1, :] - base[0]
            wide = (highs, local.shape[1])
            high_ref[e * highs : (e + 1) * highs, :] = (
                iota(I32, wide, 0) == jnp.broadcast_to(local >> (lows.bit_length() - 1), wide)
            ).astype(F32)
            wide = (lows, local.shape[1])
            low_ref[e * lows : (e + 1) * lows, :] = (
                iota(I32, wide, 0) == jnp.broadcast_to(local & (lows - 1), wide)
            ).astype(F32)
        pairs = dot(high_ref[...].astype(BF), low_ref[...].astype(BF), ((1,), (1,)))
        same = iota(I32, pairs.shape, 0) // highs == iota(I32, pairs.shape, 1) // lows
        pairs = jnp.where(same, pairs, 0.0).astype(BF)
        wide = (exp_count * lows, tok_dev)
        fold = (iota(I32, wide, 0) % lows == iota(I32, wide, 1) % lows).astype(BF)
        by_high = dot(pairs, fold, ((1,), (0,)))
        same = iota(I32, by_high.shape, 0) % highs == iota(I32, by_high.shape, 1) // lows
        by_high = jnp.where(same, by_high, 0.0).astype(BF)
        wide = (exp_count, exp_count * highs)
        fold = (iota(I32, wide, 0) == iota(I32, wide, 1) // highs).astype(BF)
        picked = dot(fold, by_high, ((1,), (0,)))
        rank = dot(picked.astype(BF), earlier(tok_dev), ((1,), (0,)))
        code_ref[...] = picked * (rank + 1.0)

    wide = (rows, exp_count)
    at = pl.program_id(0) * (rows // slots)
    repeat = (iota(I32, wide, 0) // slots + at == iota(I32, wide, 1)).astype(BF)
    code = dot(repeat, code_ref[...].astype(BF), ((1,), (0,)))
    slot = (iota(I32, code.shape, 0) % slots + 1).astype(F32)
    chosen = (code == slot).astype(F32)
    spread[...] = chosen.T.astype(BF)
    chosen = chosen.astype(BF)
    feat = tokens.shape[2]
    sent[:, :feat] = dot(chosen, tokens[0], ((1,), (0,))).astype(BF)
    sent[:, feat:] = dot(chosen, out_grad[0], ((1,), (0,))).astype(BF)


def dispatch(base, picks, tokens, out_grad, slots):
    exp_count, pick_total = picks.shape[1:]
    tok_dev, feat = tokens.shape[1:]
    lows = 16
    steps = 4
    rows = exp_count * slots // steps

    def whole(shape):
        return pl.BlockSpec(shape, lambda i: (0,) * len(shape))

    return pl.pallas_call(
        dispatch_kernel,
        grid=(steps,),
        in_specs=[
            pl.BlockSpec(memory_space=pltpu.SMEM),
            whole(picks.shape),
            whole(tokens.shape),
            whole(out_grad.shape),
        ],
        out_specs=[
            pl.BlockSpec((rows, 2 * feat), lambda i: (i, 0)),
            pl.BlockSpec((tok_dev, rows), lambda i: (0, i)),
        ],
        out_shape=[
            jax.ShapeDtypeStruct((exp_count * slots, 2 * feat), BF),
            jax.ShapeDtypeStruct((tok_dev, exp_count * slots), BF),
        ],
        scratch_shapes=[
            pltpu.VMEM((exp_count * tok_dev // lows, pick_total), F32),
            pltpu.VMEM((exp_count * lows, pick_total), F32),
            pltpu.VMEM((exp_count, tok_dev), F32),
        ],
        compiler_params=pltpu.CompilerParams(vmem_limit_bytes=60 * 1024 * 1024),
        cost_estimate=pl.CostEstimate(
            flops=4 * exp_count * slots * tok_dev * feat,
            bytes_accessed=4 * exp_count * slots * feat,
            transcendentals=0,
        ),
    )(jnp.reshape(base, (1,)).astype(I32), picks, tokens, out_grad)


def pass_kernel(rows_in, rows_grad, weight_in, weight_out, gate, grads, pre, gated, gate_slot):
    pre_act = dot(rows_in[...], weight_in[...], ((1,), (0,)))
    back = dot(rows_grad[...], weight_out[...], ((1,), (1,)))
    sig = 1.0 / (1.0 + jnp.exp(-pre_act))
    activation = (pre_act * sig).astype(BF).astype(F32)
    pre_grad = (gate[...] * back * (sig * (1.0 + pre_act * (1.0 - sig)))).astype(BF)
    gate_slot[...] = jnp.sum(activation * back, axis=1, keepdims=True)
    gated[...] = (gate[...] * activation).astype(BF)
    pre[...] = pre_grad
    grads[...] = dot(pre_grad, weight_in[...], ((1,), (1,))).astype(BF)


def expert_pass(rows, weight_in, weight_out, gate):
    count, feat, hid = rows.shape[0], weight_in.shape[0], weight_in.shape[1]
    size = min(256, count)

    def block(cols, at=0):
        return pl.BlockSpec((size, cols), lambda i: (i, at))

    def whole(shape):
        return pl.BlockSpec(shape, lambda i: (0, 0))

    return pl.pallas_call(
        pass_kernel,
        grid=(count // size,),
        in_specs=[
            block(feat),
            block(feat, 1),
            whole((feat, hid)),
            whole((hid, feat)),
            block(1),
        ],
        out_specs=[block(feat), block(hid), block(hid), block(1)],
        out_shape=[
            jax.ShapeDtypeStruct((count, feat), BF),
            jax.ShapeDtypeStruct((count, hid), BF),
            jax.ShapeDtypeStruct((count, hid), BF),
            jax.ShapeDtypeStruct((count, 1), F32),
        ],
        compiler_params=pltpu.CompilerParams(vmem_limit_bytes=48 * 1024 * 1024),
        cost_estimate=pl.CostEstimate(
            flops=6 * count * feat * hid,
            bytes_accessed=2 * (3 * count * feat + 2 * feat * hid),
            transcendentals=count * hid,
        ),
    )(rows, rows, weight_in, weight_out, gate)


def outer_kernel(scale, where, rows_in, rows_grad, pre_a, pre_b, gated_a, gated_b, *refs):
    half = pre_a.shape[1]
    gated = jnp.concatenate((gated_a[...], gated_b[...]), axis=1)
    pre = jnp.concatenate((pre_a[...], pre_b[...]), axis=1)
    out = (dot(gated, rows_grad[...], ((0,), (0,))) * scale).astype(BF)
    inn = (dot(rows_in[...], pre, ((0,), (0,))) * scale).astype(BF)
    refs[0][...], refs[2][...] = out[:half], out[half:]
    refs[1][...], refs[3][...] = inn[:, :half], inn[:, half:]


def outer(rows, pre, gated, core, scale):
    count, feat, hid = rows.shape[0], rows.shape[1] // 2, pre.shape[1] // 2
    steps = 4
    size = feat // steps
    out_block = pl.BlockSpec((hid, size), lambda i, at: (0, i))
    in_block = pl.BlockSpec((size, hid), lambda i, at: (i, 0))
    theirs = pl.BlockSpec((count, hid), lambda i, at: (0, 1 - at[0]))
    mine = pl.BlockSpec((count, hid), lambda i, at: (0, at[0]))
    out_type = jax.ShapeDtypeStruct((hid, feat), BF)
    in_type = jax.ShapeDtypeStruct((feat, hid), BF)
    parts = pl.pallas_call(
        functools.partial(outer_kernel, scale),
        grid_spec=pltpu.PrefetchScalarGridSpec(
            num_scalar_prefetch=1,
            grid=(steps,),
            in_specs=[
                pl.BlockSpec((count, size), lambda i, at: (0, i)),
                pl.BlockSpec((count, size), lambda i, at: (0, i + steps)),
                theirs,
                mine,
                theirs,
                mine,
            ],
            out_specs=[out_block, in_block] * 2,
        ),
        out_shape=[out_type, in_type] * 2,
        compiler_params=pltpu.CompilerParams(vmem_limit_bytes=48 * 1024 * 1024),
        cost_estimate=pl.CostEstimate(
            flops=8 * count * feat * hid,
            bytes_accessed=4 * (count * feat + 2 * feat * hid),
            transcendentals=0,
        ),
    )(jnp.reshape(core, (1,)).astype(I32), rows, rows, pre, pre, gated, gated)
    return parts[:2], parts[2:]


def assemble_kernel(where, *refs):
    out_pieces, in_pieces = refs[:8], refs[8:16]
    out_ref, in_ref, sems = refs[16:]
    core, near, far = where[0], where[1], where[2]
    out_rows, in_rows, in_cols = out_pieces[0].shape[0], in_pieces[0].shape[0], in_pieces[0].shape[1]
    copies = []
    for k in range(8):
        half = core if k < 4 else 1 - core
        flip_b, flip_a = k % 2, (k // 2) % 2
        a = 1 - near if flip_a else near
        b = 1 - far if flip_b else far
        row = pl.multiple_of(((half * 2 + a) * 2 + b) * out_rows, out_rows)
        place = out_ref.at[pl.ds(row, out_rows), :]
        copies.append(pltpu.make_async_copy(out_pieces[k], place, sems.at[2 * k]))
        a = 1 - far if flip_a else far
        b = 1 - near if flip_b else near
        row = pl.multiple_of((a * 2 + b) * in_rows, in_rows)
        col = pl.multiple_of(half * in_cols, in_cols)
        place = in_ref.at[pl.ds(row, in_rows), pl.ds(col, in_cols)]
        copies.append(pltpu.make_async_copy(in_pieces[k], place, sems.at[2 * k + 1]))
    for copy in copies:
        copy.start()
    for copy in copies:
        copy.wait()


def assemble(where, out_pieces, in_pieces, out_shape, in_shape):
    moved = 4 * (out_shape[0] * out_shape[1] + in_shape[0] * in_shape[1])
    return pl.pallas_call(
        assemble_kernel,
        in_specs=[pl.BlockSpec(memory_space=pltpu.SMEM)]
        + [pl.BlockSpec(memory_space=pltpu.VMEM)] * 16,
        out_specs=[pl.BlockSpec(memory_space=pl.ANY)] * 2,
        out_shape=[jax.ShapeDtypeStruct(out_shape, BF), jax.ShapeDtypeStruct(in_shape, BF)],
        scratch_shapes=[pltpu.SemaphoreType.DMA((16,))],
        compiler_params=pltpu.CompilerParams(vmem_limit_bytes=24 * 1024 * 1024),
        cost_estimate=pl.CostEstimate(flops=0, bytes_accessed=moved, transcendentals=0),
    )(where, *out_pieces, *in_pieces)


def shards(tokens, out_grad, w_in, w_out, picks, gates):
    ctx_count = lax.axis_size("ctx")
    exp_count = lax.axis_size("expert")
    core = lax.axis_index("dp")
    ctx_index = lax.axis_index("ctx")
    exp_index = lax.axis_index("expert")
    tok_dev, feat = tokens.shape[1], tokens.shape[2]
    hid = w_in.shape[2]
    pick_total = picks.shape[2]
    share = pick_total // ctx_count
    slots = ctx_count * 4
    grad_scale = (lax.axis_size("dp") * pick_total) ** (-0.5)
    lists = picks[0]
    before = earlier(tok_dev)
    tok_ids = jnp.arange(tok_dev, dtype=I32)

    def swap(rows):
        out = rows.reshape(exp_count, -1, rows.shape[1])
        out = lax.all_to_all(out, "expert", split_axis=0, concat_axis=0, tiled=True)
        return out.reshape(rows.shape)

    base = (ctx_index * exp_count + exp_index) * tok_dev
    sent, spread = dispatch(base, picks, tokens, out_grad, slots)
    arrived = swap(sent)

    own = lax.dynamic_index_in_dim(lists, exp_index, 0, keepdims=False)
    offset = own - ctx_index * (exp_count * tok_dev)
    block = offset // tok_dev
    inside = (block >= 0) & (block < exp_count)
    token = offset % tok_dev
    in_block = (inside[:, None] & (block[:, None] == jnp.arange(exp_count)[None, :])).astype(BF)
    at_token = (token[:, None] == tok_ids[None, :]).astype(BF)
    held = dot(in_block, at_token, ((0,), (0,))).astype(BF)
    rank_own = dot(held, before, ((1,), (0,))).astype(BF)
    rank_pick = jnp.sum(
        dot(in_block, rank_own, ((1,), (0,))) * at_token.astype(F32), axis=1
    ).astype(I32)
    gate_mine = gates[0, 0]
    gate_all = jnp.zeros((ctx_count, share), F32)
    gate_all = lax.dynamic_update_slice_in_dim(gate_all, gate_mine[None], ctx_index, 0)
    for step in range(1, ctx_count):
        got = lax.ppermute(gate_mine, "ctx", ring(ctx_count, step))
        gate_all = lax.dynamic_update_slice_in_dim(
            gate_all, got[None], (ctx_index - step) % ctx_count, 0
        )
    gate_all = gate_all.reshape(pick_total)

    place = jnp.where(inside, block * slots + rank_pick, -1)
    at_slot = place[:, None] == jnp.arange(exp_count * slots, dtype=I32)[None, :]
    slot_gate = jnp.sum(jnp.where(at_slot, gate_all[:, None], 0.0), axis=0)[:, None]

    row_grads, pre_grad, gated, gate_slot = expert_pass(arrived, w_in[0], w_out[0], slot_gate)
    theirs, mine = outer(arrived, pre_grad, gated, core, grad_scale)
    got = [lax.ppermute(part, "dp", SWAP) for part in theirs]
    row_grads, _ = lax.optimization_barrier((row_grads, theirs))
    returned = swap(row_grads)
    halves = [(a.astype(F32) + b.astype(F32)).astype(BF) for a, b in zip(mine, got)]

    gate_pick = jnp.sum(jnp.where(at_slot, gate_slot[:, 0][None, :], 0.0), axis=1)
    gate_rows = gate_pick.reshape(ctx_count, share)
    gate_grad = lax.dynamic_index_in_dim(gate_rows, ctx_index, 0, keepdims=False)
    for step in range(1, ctx_count):
        term = lax.dynamic_index_in_dim(
            gate_rows, (ctx_index + step) % ctx_count, 0, keepdims=False
        )
        gate_grad = gate_grad + lax.ppermute(term, "ctx", ring(ctx_count, step))

    near, far = bits(ctx_index)
    pieces, gate_grad = reduce_ctx(halves, near, far, gate_grad)
    token_total = dot(spread, returned, ((1,), (0,))).astype(BF)
    pieces = [four + tuple(lax.ppermute(term, "dp", SWAP) for term in four) for four in pieces]
    pieces, token_total = lax.optimization_barrier((pieces, token_total))
    out_total, in_total = assemble(
        jnp.stack((core, near, far)).astype(I32), *pieces, (hid, feat), (feat, hid)
    )

    return (
        token_total[None],
        in_total[None],
        out_total[None],
        gate_grad.reshape(1, 1, share),
    )


def solution(mesh):
    placed = (
        P("dp", ("ctx", "expert"), None),
        P("dp", ("ctx", "expert"), None),
        P("expert", None, None),
        P("expert", None, None),
        P("dp", None, None),
        P("dp", "expert", "ctx"),
    )
    return jax.shard_map(
        shards,
        mesh=mesh,
        in_specs=placed,
        out_specs=(
            P("dp", ("ctx", "expert"), None),
            P("expert", None, None),
            P("expert", None, None),
            P("dp", "expert", "ctx"),
        ),
        check_vma=False,
    )
```

```python
import functools

import jax
import jax.numpy as jnp
from jax import lax
from jax.experimental import pallas as pl
from jax.experimental.pallas import tpu as pltpu
from jax.sharding import PartitionSpec as P

BF = jnp.bfloat16
F32 = jnp.float32
I32 = jnp.int32
SWAP = ((0, 1), (1, 0))
NEAR = ((0, 1), (1, 0), (2, 3), (3, 2))
FAR = ((0, 3), (3, 0), (1, 2), (2, 1))


def dot(left, right, dims):
    return lax.dot_general(left, right, (dims, ((), ())), preferred_element_type=F32)


def ring(count, step):
    return [(i, (i + step) % count) for i in range(count)]


def earlier(count):
    rows = lax.broadcasted_iota(I32, (count, count), 0)
    cols = lax.broadcasted_iota(I32, (count, count), 1)
    return (rows < cols).astype(BF)


def bits(ctx_index):
    high = ctx_index // 2
    return (ctx_index % 2 + high) % 2, high


def reduce_ctx(parts, near, far, beside):
    join = lax.optimization_barrier
    plans = (((near, NEAR), (far, FAR)), ((far, FAR), (near, NEAR)))
    for step in range(2):
        sent, kept = [], []
        for part, plan in zip(parts, plans):
            keep = plan[step][0]
            size = part.shape[0] // 2
            sent.append(lax.dynamic_slice_in_dim(part, (1 - keep) * size, size))
            kept.append(lax.dynamic_slice_in_dim(part, keep * size, size))
        sent, kept = join((sent, kept))
        got = [lax.ppermute(part, "ctx", plan[step][1]) for part, plan in zip(sent, plans)]
        got, kept, beside = join((got, kept, beside))
        parts = [(a.astype(F32) + b.astype(F32)).astype(BF) for a, b in zip(kept, got)]
    parts = join(parts)
    side = [lax.ppermute(part, "ctx", plan[1][1]) for part, plan in zip(parts, plans)]
    across = [lax.ppermute(part, "ctx", plan[0][1]) for part, plan in zip(parts, plans)]
    side = join(side)
    corner = [lax.ppermute(part, "ctx", plan[0][1]) for part, plan in zip(side, plans)]
    across, corner = join((across, corner))
    return [tuple(four) for four in zip(parts, side, across, corner)], beside


def dispatch_kernel(base, picks, tokens, out_grad, sent, spread, high_ref, low_ref, code_ref):
    exp_count, tok_dev = code_ref.shape
    highs, lows = high_ref.shape[0] // exp_count, low_ref.shape[0] // exp_count
    rows = spread.shape[1]
    slots = rows * pl.num_programs(0) // exp_count
    iota = lax.broadcasted_iota

    @pl.when(pl.program_id(0) == 0)
    def _():
        for e in range(exp_count):
            local = picks[0, e : e + 1, :] - base[0]
            wide = (highs, local.shape[1])
            high_ref[e * highs : (e + 1) * highs, :] = (
                iota(I32, wide, 0) == jnp.broadcast_to(local >> (lows.bit_length() - 1), wide)
            ).astype(F32)
            wide = (lows, local.shape[1])
            low_ref[e * lows : (e + 1) * lows, :] = (
                iota(I32, wide, 0) == jnp.broadcast_to(local & (lows - 1), wide)
            ).astype(F32)
        pairs = dot(high_ref[...].astype(BF), low_ref[...].astype(BF), ((1,), (1,)))
        same = iota(I32, pairs.shape, 0) // highs == iota(I32, pairs.shape, 1) // lows
        pairs = jnp.where(same, pairs, 0.0).astype(BF)
        wide = (exp_count * lows, tok_dev)
        fold = (iota(I32, wide, 0) % lows == iota(I32, wide, 1) % lows).astype(BF)
        by_high = dot(pairs, fold, ((1,), (0,)))
        same = iota(I32, by_high.shape, 0) % highs == iota(I32, by_high.shape, 1) // lows
        by_high = jnp.where(same, by_high, 0.0).astype(BF)
        wide = (exp_count, exp_count * highs)
        fold = (iota(I32, wide, 0) == iota(I32, wide, 1) // highs).astype(BF)
        picked = dot(fold, by_high, ((1,), (0,)))
        rank = dot(picked.astype(BF), earlier(tok_dev), ((1,), (0,)))
        code_ref[...] = picked * (rank + 1.0)

    wide = (rows, exp_count)
    at = pl.program_id(0) * (rows // slots)
    repeat = (iota(I32, wide, 0) // slots + at == iota(I32, wide, 1)).astype(BF)
    code = dot(repeat, code_ref[...].astype(BF), ((1,), (0,)))
    slot = (iota(I32, code.shape, 0) % slots + 1).astype(F32)
    chosen = (code == slot).astype(F32)
    spread[...] = chosen.T.astype(BF)
    chosen = chosen.astype(BF)
    feat = tokens.shape[2]
    sent[:, :feat] = dot(chosen, tokens[0], ((1,), (0,))).astype(BF)
    sent[:, feat:] = dot(chosen, out_grad[0], ((1,), (0,))).astype(BF)


def dispatch(base, picks, tokens, out_grad, slots):
    exp_count, pick_total = picks.shape[1:]
    tok_dev, feat = tokens.shape[1:]
    lows = 16
    steps = 4
    rows = exp_count * slots // steps

    def whole(shape):
        return pl.BlockSpec(shape, lambda i: (0,) * len(shape))

    return pl.pallas_call(
        dispatch_kernel,
        grid=(steps,),
        in_specs=[
            pl.BlockSpec(memory_space=pltpu.SMEM),
            whole(picks.shape),
            whole(tokens.shape),
            whole(out_grad.shape),
        ],
        out_specs=[
            pl.BlockSpec((rows, 2 * feat), lambda i: (i, 0)),
            pl.BlockSpec((tok_dev, rows), lambda i: (0, i)),
        ],
        out_shape=[
            jax.ShapeDtypeStruct((exp_count * slots, 2 * feat), BF),
            jax.ShapeDtypeStruct((tok_dev, exp_count * slots), BF),
        ],
        scratch_shapes=[
            pltpu.VMEM((exp_count * tok_dev // lows, pick_total), F32),
            pltpu.VMEM((exp_count * lows, pick_total), F32),
            pltpu.VMEM((exp_count, tok_dev), F32),
        ],
        compiler_params=pltpu.CompilerParams(vmem_limit_bytes=60 * 1024 * 1024),
        cost_estimate=pl.CostEstimate(
            flops=4 * exp_count * slots * tok_dev * feat,
            bytes_accessed=4 * exp_count * slots * feat,
            transcendentals=0,
        ),
    )(jnp.reshape(base, (1,)).astype(I32), picks, tokens, out_grad)


def expert_kernel(scale, core, gate, in_hbm, out_hbm, rows, gate_slot, *refs):
    outs, refs = refs[:5], refs[5:]
    weight_in, in_turned, weight_out, out_turned, held = refs[:5]
    grads, out_theirs, in_theirs, out_mine, in_mine, pre, gated, in_sems, out_sems = refs[5:]
    count, feat = grads.shape
    hid = pre.shape[1]
    chunks = 2
    size = count // chunks
    copy_of = pltpu.make_async_copy

    def chunk(i, part):
        at = (pl.ds(i * size, size), pl.ds(part * feat, feat))
        return copy_of(rows.at[at], held.at[at], in_sems.at[2 * i + part])

    loads = [
        copy_of(out_hbm, weight_out, in_sems.at[2 * chunks]),
        copy_of(in_hbm, weight_in, in_sems.at[2 * chunks + 1]),
        chunk(0, 0),
        chunk(0, 1),
        chunk(1, 0),
        chunk(1, 1),
    ]
    for load in loads:
        load.start()
    sent = []

    def send(source, target):
        sent.append(copy_of(source, target, out_sems.at[len(sent)]))
        sent[-1].start()

    lanes = 128
    wide = jnp.broadcast_to(gate[...], (lanes, count)).T
    wide = jnp.concatenate([wide] * (hid // lanes), axis=1)
    loads[0].wait()
    out_turned[...] = weight_out[...].T
    loads[1].wait()
    in_turned[...] = weight_in[...].T
    for i in range(chunks):
        at = slice(i * size, (i + 1) * size)
        loads[2 + 2 * i].wait()
        pre_act = dot(held[at, :feat], weight_in[...], ((1,), (0,)))
        loads[3 + 2 * i].wait()
        back = dot(held[at, feat:], out_turned[...], ((1,), (0,)))
        sig = 1.0 / (1.0 + jnp.exp(-pre_act))
        activation = (pre_act * sig).astype(BF).astype(F32)
        terms = activation * back
        terms = sum(terms[:, k : k + lanes] for k in range(0, hid, lanes))
        gate_slot[:, at] = jnp.sum(terms.T, axis=0, keepdims=True)
        gated[at, :] = (wide[at, :] * activation).astype(BF)
        pre_grad = (wide[at, :] * back * (sig * (1.0 + pre_act * (1.0 - sig)))).astype(BF)
        pre[at, :] = pre_grad
        grads[at, :] = dot(pre_grad, in_turned[...], ((1,), (0,))).astype(BF)
        place = pl.ds(i * size, size)
        send(grads.at[place, :], outs[0].at[place, :])

    def theirs_first(ref):
        low, high = ref[:, : hid // 2], ref[:, hid // 2 :]
        first = core[0] == 0
        return jnp.concatenate((jnp.where(first, high, low), jnp.where(first, low, high)), axis=1)

    gated_pair, pre_pair = theirs_first(gated), theirs_first(pre)
    width = 512
    for first in range(0, feat, width):
        at = slice(first, first + width)
        grad_at = slice(feat + first, feat + first + width)
        out = (dot(gated_pair, held[:, grad_at], ((0,), (0,))) * scale).astype(BF)
        out_theirs[:, at], out_mine[:, at] = out[: hid // 2], out[hid // 2 :]
        inn = (dot(held[:, at], pre_pair, ((0,), (0,))) * scale).astype(BF)
        in_theirs[at, :], in_mine[at, :] = inn[:, : hid // 2], inn[:, hid // 2 :]
        place = pl.ds(first, width)
        send(out_theirs.at[:, place], outs[1].at[:, place])
        send(in_theirs.at[place, :], outs[2].at[place, :])
        send(out_mine.at[:, place], outs[3].at[:, place])
        send(in_mine.at[place, :], outs[4].at[place, :])
    for copy in sent:
        copy.wait()


def expert_pass(rows, weight_in, weight_out, gate, core, scale):
    count, feat, hid = rows.shape[0], weight_in.shape[0], weight_in.shape[1]
    vmem = pl.BlockSpec(memory_space=pltpu.VMEM)
    anywhere = pl.BlockSpec(memory_space=pl.ANY)
    shapes = [(count, feat)] + [(hid // 2, feat), (feat, hid // 2)] * 2
    held = [(feat, hid), (hid, feat), (hid, feat), (feat, hid), rows.shape]
    held += shapes + [(count, hid)] * 2
    gate_slot, grads, *parts = pl.pallas_call(
        functools.partial(expert_kernel, scale),
        in_specs=[pl.BlockSpec(memory_space=pltpu.SMEM), vmem] + [anywhere] * 3,
        out_specs=[vmem] + [anywhere] * 5,
        out_shape=[jax.ShapeDtypeStruct((1, count), F32)]
        + [jax.ShapeDtypeStruct(shape, BF) for shape in shapes],
        scratch_shapes=[pltpu.VMEM(shape, BF) for shape in held]
        + [pltpu.SemaphoreType.DMA((6,)), pltpu.SemaphoreType.DMA((18,))],
        compiler_params=pltpu.CompilerParams(vmem_limit_bytes=58 * 1024 * 1024),
        cost_estimate=pl.CostEstimate(
            flops=10 * count * feat * hid,
            bytes_accessed=4 * (count * feat + feat * hid),
            transcendentals=count * hid,
        ),
    )(jnp.reshape(core, (1,)).astype(I32), gate, weight_in, weight_out, rows)
    return grads, gate_slot, parts[:2], parts[2:]


def assemble_kernel(where, *refs):
    out_pieces, in_pieces = refs[:8], refs[8:16]
    out_ref, in_ref, sems = refs[16:]
    core, near, far = where[0], where[1], where[2]
    out_rows, in_rows, in_cols = out_pieces[0].shape[0], in_pieces[0].shape[0], in_pieces[0].shape[1]
    copies = []
    for k in range(8):
        half = core if k < 4 else 1 - core
        flip_b, flip_a = k % 2, (k // 2) % 2
        a = 1 - near if flip_a else near
        b = 1 - far if flip_b else far
        row = pl.multiple_of(((half * 2 + a) * 2 + b) * out_rows, out_rows)
        place = out_ref.at[pl.ds(row, out_rows), :]
        copies.append(pltpu.make_async_copy(out_pieces[k], place, sems.at[2 * k]))
        a = 1 - far if flip_a else far
        b = 1 - near if flip_b else near
        row = pl.multiple_of((a * 2 + b) * in_rows, in_rows)
        col = pl.multiple_of(half * in_cols, in_cols)
        place = in_ref.at[pl.ds(row, in_rows), pl.ds(col, in_cols)]
        copies.append(pltpu.make_async_copy(in_pieces[k], place, sems.at[2 * k + 1]))
    for copy in copies:
        copy.start()
    for copy in copies:
        copy.wait()


def assemble(where, out_pieces, in_pieces, out_shape, in_shape):
    moved = 4 * (out_shape[0] * out_shape[1] + in_shape[0] * in_shape[1])
    return pl.pallas_call(
        assemble_kernel,
        in_specs=[pl.BlockSpec(memory_space=pltpu.SMEM)]
        + [pl.BlockSpec(memory_space=pltpu.VMEM)] * 16,
        out_specs=[pl.BlockSpec(memory_space=pl.ANY)] * 2,
        out_shape=[jax.ShapeDtypeStruct(out_shape, BF), jax.ShapeDtypeStruct(in_shape, BF)],
        scratch_shapes=[pltpu.SemaphoreType.DMA((16,))],
        compiler_params=pltpu.CompilerParams(vmem_limit_bytes=24 * 1024 * 1024),
        cost_estimate=pl.CostEstimate(flops=0, bytes_accessed=moved, transcendentals=0),
    )(where, *out_pieces, *in_pieces)


def shards(tokens, out_grad, w_in, w_out, picks, gates):
    ctx_count = lax.axis_size("ctx")
    exp_count = lax.axis_size("expert")
    core = lax.axis_index("dp")
    ctx_index = lax.axis_index("ctx")
    exp_index = lax.axis_index("expert")
    tok_dev, feat = tokens.shape[1], tokens.shape[2]
    hid = w_in.shape[2]
    pick_total = picks.shape[2]
    share = pick_total // ctx_count
    slots = ctx_count * 4
    grad_scale = (lax.axis_size("dp") * pick_total) ** (-0.5)
    lists = picks[0]
    before = earlier(tok_dev)
    tok_ids = jnp.arange(tok_dev, dtype=I32)

    def swap(rows):
        out = rows.reshape(exp_count, -1, rows.shape[1])
        out = lax.all_to_all(out, "expert", split_axis=0, concat_axis=0, tiled=True)
        return out.reshape(rows.shape)

    base = (ctx_index * exp_count + exp_index) * tok_dev
    sent, spread = dispatch(base, picks, tokens, out_grad, slots)
    arrived = swap(sent)

    own = lax.dynamic_index_in_dim(lists, exp_index, 0, keepdims=False)
    offset = own - ctx_index * (exp_count * tok_dev)
    block = offset // tok_dev
    inside = (block >= 0) & (block < exp_count)
    token = offset % tok_dev
    in_block = (inside[:, None] & (block[:, None] == jnp.arange(exp_count)[None, :])).astype(BF)
    at_token = (token[:, None] == tok_ids[None, :]).astype(BF)
    held = dot(in_block, at_token, ((0,), (0,))).astype(BF)
    rank_own = dot(held, before, ((1,), (0,))).astype(BF)
    rank_pick = jnp.sum(
        dot(in_block, rank_own, ((1,), (0,))) * at_token.astype(F32), axis=1
    ).astype(I32)
    gate_mine = gates[0, 0]
    gate_all = jnp.zeros((ctx_count, share), F32)
    gate_all = lax.dynamic_update_slice_in_dim(gate_all, gate_mine[None], ctx_index, 0)
    for step in range(1, ctx_count):
        got = lax.ppermute(gate_mine, "ctx", ring(ctx_count, step))
        gate_all = lax.dynamic_update_slice_in_dim(
            gate_all, got[None], (ctx_index - step) % ctx_count, 0
        )
    gate_all = gate_all.reshape(pick_total)

    place = jnp.where(inside, block * slots + rank_pick, -1)
    at_slot = place[:, None] == jnp.arange(exp_count * slots, dtype=I32)[None, :]
    slot_gate = jnp.sum(jnp.where(at_slot, gate_all[:, None], 0.0), axis=0)[None, :]

    row_grads, gate_slot, theirs, mine = expert_pass(
        arrived, w_in[0], w_out[0], slot_gate, core, grad_scale
    )
    got = [lax.ppermute(part, "dp", SWAP) for part in theirs]
    row_grads, _ = lax.optimization_barrier((row_grads, theirs))
    returned = swap(row_grads)
    halves = [(a.astype(F32) + b.astype(F32)).astype(BF) for a, b in zip(mine, got)]

    gate_pick = jnp.sum(jnp.where(at_slot, gate_slot, 0.0), axis=1)
    gate_rows = gate_pick.reshape(ctx_count, share)
    gate_grad = lax.dynamic_index_in_dim(gate_rows, ctx_index, 0, keepdims=False)
    for step in range(1, ctx_count):
        term = lax.dynamic_index_in_dim(
            gate_rows, (ctx_index + step) % ctx_count, 0, keepdims=False
        )
        gate_grad = gate_grad + lax.ppermute(term, "ctx", ring(ctx_count, step))

    near, far = bits(ctx_index)
    pieces, gate_grad = reduce_ctx(halves, near, far, gate_grad)
    token_total = dot(spread, returned, ((1,), (0,))).astype(BF)
    pieces = [four + tuple(lax.ppermute(term, "dp", SWAP) for term in four) for four in pieces]
    pieces, token_total = lax.optimization_barrier((pieces, token_total))
    out_total, in_total = assemble(
        jnp.stack((core, near, far)).astype(I32), *pieces, (hid, feat), (feat, hid)
    )

    return (
        token_total[None],
        in_total[None],
        out_total[None],
        gate_grad.reshape(1, 1, share),
    )


def solution(mesh):
    placed = (
        P("dp", ("ctx", "expert"), None),
        P("dp", ("ctx", "expert"), None),
        P("expert", None, None),
        P("expert", None, None),
        P("dp", None, None),
        P("dp", "expert", "ctx"),
    )
    return jax.shard_map(
        shards,
        mesh=mesh,
        in_specs=placed,
        out_specs=(
            P("dp", ("ctx", "expert"), None),
            P("expert", None, None),
            P("expert", None, None),
            P("dp", "expert", "ctx"),
        ),
        check_vma=False,
    )
```

```python
import functools

import jax
import jax.numpy as jnp
from jax import lax
from jax.experimental import pallas as pl
from jax.experimental.pallas import tpu as pltpu
from jax.sharding import PartitionSpec as P

BF = jnp.bfloat16
F32 = jnp.float32
I32 = jnp.int32
SWAP = ((0, 1), (1, 0))
NEAR = ((0, 1), (1, 0), (2, 3), (3, 2))
FAR = ((0, 3), (3, 0), (1, 2), (2, 1))


def dot(left, right, dims):
    return lax.dot_general(left, right, (dims, ((), ())), preferred_element_type=F32)


def ring(count, step):
    return [(i, (i + step) % count) for i in range(count)]


def earlier(count):
    rows = lax.broadcasted_iota(I32, (count, count), 0)
    cols = lax.broadcasted_iota(I32, (count, count), 1)
    return (rows < cols).astype(BF)


def bits(ctx_index):
    high = ctx_index // 2
    return (ctx_index % 2 + high) % 2, high


def reduce_ctx(parts, near, far, beside):
    join = lax.optimization_barrier
    plans = (((near, NEAR), (far, FAR)), ((far, FAR), (near, NEAR)))
    for step in range(2):
        sent, kept = [], []
        for part, plan in zip(parts, plans):
            keep = plan[step][0]
            size = part.shape[0] // 2
            sent.append(lax.dynamic_slice_in_dim(part, (1 - keep) * size, size))
            kept.append(lax.dynamic_slice_in_dim(part, keep * size, size))
        sent, kept = join((sent, kept))
        got = [lax.ppermute(part, "ctx", plan[step][1]) for part, plan in zip(sent, plans)]
        got, kept, beside = join((got, kept, beside))
        parts = [(a.astype(F32) + b.astype(F32)).astype(BF) for a, b in zip(kept, got)]
    parts = join(parts)
    side = [lax.ppermute(part, "ctx", plan[1][1]) for part, plan in zip(parts, plans)]
    across = [lax.ppermute(part, "ctx", plan[0][1]) for part, plan in zip(parts, plans)]
    side = join(side)
    corner = [lax.ppermute(part, "ctx", plan[0][1]) for part, plan in zip(side, plans)]
    across, corner = join((across, corner))
    return [tuple(four) for four in zip(parts, side, across, corner)], beside


def dispatch_kernel(base, picks, tokens, out_grad, sent, spread, high_ref, low_ref, code_ref):
    exp_count, tok_dev = code_ref.shape
    highs, lows = high_ref.shape[0] // exp_count, low_ref.shape[0] // exp_count
    rows = spread.shape[1]
    slots = rows * pl.num_programs(0) // exp_count
    iota = lax.broadcasted_iota

    @pl.when(pl.program_id(0) == 0)
    def _():
        for e in range(exp_count):
            local = picks[0, e : e + 1, :] - base[0]
            wide = (highs, local.shape[1])
            high_ref[e * highs : (e + 1) * highs, :] = (
                iota(I32, wide, 0) == jnp.broadcast_to(local >> (lows.bit_length() - 1), wide)
            ).astype(F32)
            wide = (lows, local.shape[1])
            low_ref[e * lows : (e + 1) * lows, :] = (
                iota(I32, wide, 0) == jnp.broadcast_to(local & (lows - 1), wide)
            ).astype(F32)
        pairs = dot(high_ref[...].astype(BF), low_ref[...].astype(BF), ((1,), (1,)))
        same = iota(I32, pairs.shape, 0) // highs == iota(I32, pairs.shape, 1) // lows
        pairs = jnp.where(same, pairs, 0.0).astype(BF)
        wide = (exp_count * lows, tok_dev)
        fold = (iota(I32, wide, 0) % lows == iota(I32, wide, 1) % lows).astype(BF)
        by_high = dot(pairs, fold, ((1,), (0,)))
        same = iota(I32, by_high.shape, 0) % highs == iota(I32, by_high.shape, 1) // lows
        by_high = jnp.where(same, by_high, 0.0).astype(BF)
        wide = (exp_count, exp_count * highs)
        fold = (iota(I32, wide, 0) == iota(I32, wide, 1) // highs).astype(BF)
        picked = dot(fold, by_high, ((1,), (0,)))
        rank = dot(picked.astype(BF), earlier(tok_dev), ((1,), (0,)))
        code_ref[...] = picked * (rank + 1.0)

    wide = (rows, exp_count)
    at = pl.program_id(0) * (rows // slots)
    repeat = (iota(I32, wide, 0) // slots + at == iota(I32, wide, 1)).astype(BF)
    code = dot(repeat, code_ref[...].astype(BF), ((1,), (0,)))
    slot = (iota(I32, code.shape, 0) % slots + 1).astype(F32)
    chosen = (code == slot).astype(F32)
    spread[...] = chosen.T.astype(BF)
    chosen = chosen.astype(BF)
    feat = tokens.shape[2]
    sent[:, :feat] = dot(chosen, tokens[0], ((1,), (0,))).astype(BF)
    sent[:, feat:] = dot(chosen, out_grad[0], ((1,), (0,))).astype(BF)


def dispatch(base, picks, tokens, out_grad, slots):
    exp_count, pick_total = picks.shape[1:]
    tok_dev, feat = tokens.shape[1:]
    lows = 16
    steps = 2
    rows = exp_count * slots // steps

    def whole(shape):
        return pl.BlockSpec(shape, lambda i: (0,) * len(shape))

    return pl.pallas_call(
        dispatch_kernel,
        grid=(steps,),
        in_specs=[
            pl.BlockSpec(memory_space=pltpu.SMEM),
            whole(picks.shape),
            whole(tokens.shape),
            whole(out_grad.shape),
        ],
        out_specs=[
            pl.BlockSpec((rows, 2 * feat), lambda i: (i, 0)),
            pl.BlockSpec((tok_dev, rows), lambda i: (0, i)),
        ],
        out_shape=[
            jax.ShapeDtypeStruct((exp_count * slots, 2 * feat), BF),
            jax.ShapeDtypeStruct((tok_dev, exp_count * slots), BF),
        ],
        scratch_shapes=[
            pltpu.VMEM((exp_count * tok_dev // lows, pick_total), F32),
            pltpu.VMEM((exp_count * lows, pick_total), F32),
            pltpu.VMEM((exp_count, tok_dev), F32),
        ],
        compiler_params=pltpu.CompilerParams(vmem_limit_bytes=60 * 1024 * 1024),
        cost_estimate=pl.CostEstimate(
            flops=4 * exp_count * slots * tok_dev * feat,
            bytes_accessed=4 * exp_count * slots * feat,
            transcendentals=0,
        ),
    )(jnp.reshape(base, (1,)).astype(I32), picks, tokens, out_grad)


def expert_kernel(scale, core, gate, in_hbm, out_hbm, rows, gate_slot, *refs):
    outs, refs = refs[:5], refs[5:]
    weight_in, in_turned, weight_out, out_turned, held = refs[:5]
    grads, out_theirs, in_theirs, out_mine, in_mine, pre, gated, in_sems, out_sems = refs[5:]
    count, feat = grads.shape
    hid = pre.shape[1]
    chunks = 2
    size = count // chunks
    copy_of = pltpu.make_async_copy

    def chunk(i, part):
        at = (pl.ds(i * size, size), pl.ds(part * feat, feat))
        return copy_of(rows.at[at], held.at[at], in_sems.at[2 * i + part])

    loads = [
        copy_of(out_hbm, weight_out, in_sems.at[2 * chunks]),
        copy_of(in_hbm, weight_in, in_sems.at[2 * chunks + 1]),
        chunk(0, 0),
        chunk(0, 1),
        chunk(1, 0),
        chunk(1, 1),
    ]
    for load in loads:
        load.start()
    sent = []

    def send(source, target):
        sent.append(copy_of(source, target, out_sems.at[len(sent)]))
        sent[-1].start()

    lanes = 128
    wide = jnp.broadcast_to(gate[...], (lanes, count)).T
    wide = jnp.concatenate([wide] * (hid // lanes), axis=1)
    loads[0].wait()
    out_turned[...] = weight_out[...].T
    loads[1].wait()
    in_turned[...] = weight_in[...].T
    for i in range(chunks):
        at = slice(i * size, (i + 1) * size)
        loads[2 + 2 * i].wait()
        pre_act = dot(held[at, :feat], weight_in[...], ((1,), (0,)))
        loads[3 + 2 * i].wait()
        back = dot(held[at, feat:], out_turned[...], ((1,), (0,)))
        sig = 1.0 / (1.0 + jnp.exp(-pre_act))
        activation = (pre_act * sig).astype(BF).astype(F32)
        terms = activation * back
        terms = sum(terms[:, k : k + lanes] for k in range(0, hid, lanes))
        gate_slot[:, at] = jnp.sum(terms.T, axis=0, keepdims=True)
        gated[at, :] = (wide[at, :] * activation).astype(BF)
        pre_grad = (wide[at, :] * back * (sig * (1.0 + pre_act * (1.0 - sig)))).astype(BF)
        pre[at, :] = pre_grad
        grads[at, :] = dot(pre_grad, in_turned[...], ((1,), (0,))).astype(BF)
        place = pl.ds(i * size, size)
        send(grads.at[place, :], outs[0].at[place, :])

    def theirs_first(ref):
        low, high = ref[:, : hid // 2], ref[:, hid // 2 :]
        first = core[0] == 0
        return jnp.concatenate((jnp.where(first, high, low), jnp.where(first, low, high)), axis=1)

    gated_pair, pre_pair = theirs_first(gated), theirs_first(pre)
    width = 512
    for first in range(0, feat, width):
        at = slice(first, first + width)
        grad_at = slice(feat + first, feat + first + width)
        out = (dot(gated_pair, held[:, grad_at], ((0,), (0,))) * scale).astype(BF)
        out_theirs[:, at], out_mine[:, at] = out[: hid // 2], out[hid // 2 :]
        inn = (dot(held[:, at], pre_pair, ((0,), (0,))) * scale).astype(BF)
        in_theirs[at, :], in_mine[at, :] = inn[:, : hid // 2], inn[:, hid // 2 :]
        place = pl.ds(first, width)
        send(out_theirs.at[:, place], outs[1].at[:, place])
        send(in_theirs.at[place, :], outs[2].at[place, :])
        send(out_mine.at[:, place], outs[3].at[:, place])
        send(in_mine.at[place, :], outs[4].at[place, :])
    for copy in sent:
        copy.wait()


def expert_pass(rows, weight_in, weight_out, gate, core, scale):
    count, feat, hid = rows.shape[0], weight_in.shape[0], weight_in.shape[1]
    vmem = pl.BlockSpec(memory_space=pltpu.VMEM)
    anywhere = pl.BlockSpec(memory_space=pl.ANY)
    shapes = [(count, feat)] + [(hid // 2, feat), (feat, hid // 2)] * 2
    held = [(feat, hid), (hid, feat), (hid, feat), (feat, hid), rows.shape]
    held += shapes + [(count, hid)] * 2
    gate_slot, grads, *parts = pl.pallas_call(
        functools.partial(expert_kernel, scale),
        in_specs=[pl.BlockSpec(memory_space=pltpu.SMEM), vmem] + [anywhere] * 3,
        out_specs=[vmem] + [anywhere] * 5,
        out_shape=[jax.ShapeDtypeStruct((1, count), F32)]
        + [jax.ShapeDtypeStruct(shape, BF) for shape in shapes],
        scratch_shapes=[pltpu.VMEM(shape, BF) for shape in held]
        + [pltpu.SemaphoreType.DMA((6,)), pltpu.SemaphoreType.DMA((18,))],
        compiler_params=pltpu.CompilerParams(vmem_limit_bytes=58 * 1024 * 1024),
        cost_estimate=pl.CostEstimate(
            flops=10 * count * feat * hid,
            bytes_accessed=4 * (count * feat + feat * hid),
            transcendentals=count * hid,
        ),
    )(jnp.reshape(core, (1,)).astype(I32), gate, weight_in, weight_out, rows)
    return grads, gate_slot, parts[:2], parts[2:]


def assemble_kernel(where, *refs):
    out_pieces, in_pieces = refs[:8], refs[8:16]
    out_ref, in_ref, sems = refs[16:]
    core, near, far = where[0], where[1], where[2]
    out_rows, in_rows, in_cols = out_pieces[0].shape[0], in_pieces[0].shape[0], in_pieces[0].shape[1]
    copies = []
    for k in range(8):
        half = core if k < 4 else 1 - core
        flip_b, flip_a = k % 2, (k // 2) % 2
        a = 1 - near if flip_a else near
        b = 1 - far if flip_b else far
        row = pl.multiple_of(((half * 2 + a) * 2 + b) * out_rows, out_rows)
        place = out_ref.at[pl.ds(row, out_rows), :]
        copies.append(pltpu.make_async_copy(out_pieces[k], place, sems.at[2 * k]))
        a = 1 - far if flip_a else far
        b = 1 - near if flip_b else near
        row = pl.multiple_of((a * 2 + b) * in_rows, in_rows)
        col = pl.multiple_of(half * in_cols, in_cols)
        place = in_ref.at[pl.ds(row, in_rows), pl.ds(col, in_cols)]
        copies.append(pltpu.make_async_copy(in_pieces[k], place, sems.at[2 * k + 1]))
    for copy in copies:
        copy.start()
    for copy in copies:
        copy.wait()


def assemble(where, out_pieces, in_pieces, out_shape, in_shape):
    moved = 4 * (out_shape[0] * out_shape[1] + in_shape[0] * in_shape[1])
    return pl.pallas_call(
        assemble_kernel,
        in_specs=[pl.BlockSpec(memory_space=pltpu.SMEM)]
        + [pl.BlockSpec(memory_space=pltpu.VMEM)] * 16,
        out_specs=[pl.BlockSpec(memory_space=pl.ANY)] * 2,
        out_shape=[jax.ShapeDtypeStruct(out_shape, BF), jax.ShapeDtypeStruct(in_shape, BF)],
        scratch_shapes=[pltpu.SemaphoreType.DMA((16,))],
        compiler_params=pltpu.CompilerParams(vmem_limit_bytes=24 * 1024 * 1024),
        cost_estimate=pl.CostEstimate(flops=0, bytes_accessed=moved, transcendentals=0),
    )(where, *out_pieces, *in_pieces)


def shards(tokens, out_grad, w_in, w_out, picks, gates):
    ctx_count = lax.axis_size("ctx")
    exp_count = lax.axis_size("expert")
    core = lax.axis_index("dp")
    ctx_index = lax.axis_index("ctx")
    exp_index = lax.axis_index("expert")
    tok_dev, feat = tokens.shape[1], tokens.shape[2]
    hid = w_in.shape[2]
    pick_total = picks.shape[2]
    share = pick_total // ctx_count
    slots = ctx_count * 4
    grad_scale = (lax.axis_size("dp") * pick_total) ** (-0.5)
    lists = picks[0]
    before = earlier(tok_dev)
    tok_ids = jnp.arange(tok_dev, dtype=I32)

    def swap(rows):
        out = rows.reshape(exp_count, -1, rows.shape[1])
        out = lax.all_to_all(out, "expert", split_axis=0, concat_axis=0, tiled=True)
        return out.reshape(rows.shape)

    base = (ctx_index * exp_count + exp_index) * tok_dev
    sent, spread = dispatch(base, picks, tokens, out_grad, slots)
    arrived = swap(sent)

    own = lax.dynamic_index_in_dim(lists, exp_index, 0, keepdims=False)
    offset = own - ctx_index * (exp_count * tok_dev)
    block = offset // tok_dev
    inside = (block >= 0) & (block < exp_count)
    token = offset % tok_dev
    in_block = (inside[:, None] & (block[:, None] == jnp.arange(exp_count)[None, :])).astype(BF)
    at_token = (token[:, None] == tok_ids[None, :]).astype(BF)
    held = dot(in_block, at_token, ((0,), (0,))).astype(BF)
    rank_own = dot(held, before, ((1,), (0,))).astype(BF)
    rank_pick = jnp.sum(
        dot(in_block, rank_own, ((1,), (0,))) * at_token.astype(F32), axis=1
    ).astype(I32)
    gate_mine = gates[0, 0]
    gate_all = jnp.zeros((ctx_count, share), F32)
    gate_all = lax.dynamic_update_slice_in_dim(gate_all, gate_mine[None], ctx_index, 0)
    for step in range(1, ctx_count):
        got = lax.ppermute(gate_mine, "ctx", ring(ctx_count, step))
        gate_all = lax.dynamic_update_slice_in_dim(
            gate_all, got[None], (ctx_index - step) % ctx_count, 0
        )
    gate_all = gate_all.reshape(pick_total)

    place = jnp.where(inside, block * slots + rank_pick, -1)
    at_slot = place[:, None] == jnp.arange(exp_count * slots, dtype=I32)[None, :]
    slot_gate = jnp.sum(jnp.where(at_slot, gate_all[:, None], 0.0), axis=0)[None, :]

    row_grads, gate_slot, theirs, mine = expert_pass(
        arrived, w_in[0], w_out[0], slot_gate, core, grad_scale
    )
    got = [lax.ppermute(part, "dp", SWAP) for part in theirs]
    row_grads, _ = lax.optimization_barrier((row_grads, theirs))
    returned = swap(row_grads)
    halves = [(a.astype(F32) + b.astype(F32)).astype(BF) for a, b in zip(mine, got)]

    gate_pick = jnp.sum(jnp.where(at_slot, gate_slot, 0.0), axis=1)
    gate_rows = gate_pick.reshape(ctx_count, share)
    gate_grad = lax.dynamic_index_in_dim(gate_rows, ctx_index, 0, keepdims=False)
    for step in range(1, ctx_count):
        term = lax.dynamic_index_in_dim(
            gate_rows, (ctx_index + step) % ctx_count, 0, keepdims=False
        )
        gate_grad = gate_grad + lax.ppermute(term, "ctx", ring(ctx_count, step))

    near, far = bits(ctx_index)
    pieces, gate_grad = reduce_ctx(halves, near, far, gate_grad)
    token_total = dot(spread, returned, ((1,), (0,))).astype(BF)
    pieces = [four + tuple(lax.ppermute(term, "dp", SWAP) for term in four) for four in pieces]
    pieces, token_total = lax.optimization_barrier((pieces, token_total))
    out_total, in_total = assemble(
        jnp.stack((core, near, far)).astype(I32), *pieces, (hid, feat), (feat, hid)
    )

    return (
        token_total[None],
        in_total[None],
        out_total[None],
        gate_grad.reshape(1, 1, share),
    )


def solution(mesh):
    placed = (
        P("dp", ("ctx", "expert"), None),
        P("dp", ("ctx", "expert"), None),
        P("expert", None, None),
        P("expert", None, None),
        P("dp", None, None),
        P("dp", "expert", "ctx"),
    )
    return jax.shard_map(
        shards,
        mesh=mesh,
        in_specs=placed,
        out_specs=(
            P("dp", ("ctx", "expert"), None),
            P("expert", None, None),
            P("expert", None, None),
            P("dp", "expert", "ctx"),
        ),
        check_vma=False,
    )
```

```python
import functools

import jax
import jax.numpy as jnp
from jax import lax
from jax.experimental import pallas as pl
from jax.experimental.pallas import tpu as pltpu
from jax.sharding import PartitionSpec as P

BF = jnp.bfloat16
F32 = jnp.float32
I32 = jnp.int32
SWAP = ((0, 1), (1, 0))
NEAR = ((0, 1), (1, 0), (2, 3), (3, 2))
FAR = ((0, 3), (3, 0), (1, 2), (2, 1))


def dot(left, right, dims):
    return lax.dot_general(left, right, (dims, ((), ())), preferred_element_type=F32)


def ring(count, step):
    return [(i, (i + step) % count) for i in range(count)]


def earlier(count):
    rows = lax.broadcasted_iota(I32, (count, count), 0)
    cols = lax.broadcasted_iota(I32, (count, count), 1)
    return (rows < cols).astype(BF)


def bits(ctx_index):
    high = ctx_index // 2
    return (ctx_index % 2 + high) % 2, high


def reduce_ctx(parts, near, far, beside):
    join = lax.optimization_barrier
    plans = (((near, NEAR), (far, FAR)), ((far, FAR), (near, NEAR)))
    for step in range(2):
        sent, kept = [], []
        for part, plan in zip(parts, plans):
            keep = plan[step][0]
            size = part.shape[0] // 2
            sent.append(lax.dynamic_slice_in_dim(part, (1 - keep) * size, size))
            kept.append(lax.dynamic_slice_in_dim(part, keep * size, size))
        sent, kept = join((sent, kept))
        got = [lax.ppermute(part, "ctx", plan[step][1]) for part, plan in zip(sent, plans)]
        got, kept, beside = join((got, kept, beside))
        parts = [(a.astype(F32) + b.astype(F32)).astype(BF) for a, b in zip(kept, got)]
    parts = join(parts)
    side = [lax.ppermute(part, "ctx", plan[1][1]) for part, plan in zip(parts, plans)]
    across = [lax.ppermute(part, "ctx", plan[0][1]) for part, plan in zip(parts, plans)]
    side = join(side)
    corner = [lax.ppermute(part, "ctx", plan[0][1]) for part, plan in zip(side, plans)]
    across, corner = join((across, corner))
    return [tuple(four) for four in zip(parts, side, across, corner)], beside


def dispatch_kernel(base, picks, tokens, out_grad, sent, spread, high_ref, low_ref, code_ref):
    exp_count, tok_dev = code_ref.shape
    highs, lows = high_ref.shape[0] // exp_count, low_ref.shape[0] // exp_count
    rows = spread.shape[1]
    slots = rows * pl.num_programs(0) // exp_count
    iota = lax.broadcasted_iota

    @pl.when(pl.program_id(0) == 0)
    def _():
        for e in range(exp_count):
            local = picks[0, e : e + 1, :] - base[0]
            wide = (highs, local.shape[1])
            high_ref[e * highs : (e + 1) * highs, :] = (
                iota(I32, wide, 0) == jnp.broadcast_to(local >> (lows.bit_length() - 1), wide)
            ).astype(F32)
            wide = (lows, local.shape[1])
            low_ref[e * lows : (e + 1) * lows, :] = (
                iota(I32, wide, 0) == jnp.broadcast_to(local & (lows - 1), wide)
            ).astype(F32)
        pairs = dot(high_ref[...].astype(BF), low_ref[...].astype(BF), ((1,), (1,)))
        same = iota(I32, pairs.shape, 0) // highs == iota(I32, pairs.shape, 1) // lows
        pairs = jnp.where(same, pairs, 0.0).astype(BF)
        wide = (exp_count * lows, tok_dev)
        fold = (iota(I32, wide, 0) % lows == iota(I32, wide, 1) % lows).astype(BF)
        by_high = dot(pairs, fold, ((1,), (0,)))
        same = iota(I32, by_high.shape, 0) % highs == iota(I32, by_high.shape, 1) // lows
        by_high = jnp.where(same, by_high, 0.0).astype(BF)
        wide = (exp_count, exp_count * highs)
        fold = (iota(I32, wide, 0) == iota(I32, wide, 1) // highs).astype(BF)
        picked = dot(fold, by_high, ((1,), (0,)))
        rank = dot(picked.astype(BF), earlier(tok_dev), ((1,), (0,)))
        code_ref[...] = picked * (rank + 1.0)

    wide = (rows, exp_count)
    at = pl.program_id(0) * (rows // slots)
    repeat = (iota(I32, wide, 0) // slots + at == iota(I32, wide, 1)).astype(BF)
    code = dot(repeat, code_ref[...].astype(BF), ((1,), (0,)))
    slot = (iota(I32, code.shape, 0) % slots + 1).astype(F32)
    chosen = (code == slot).astype(F32)
    spread[...] = chosen.T.astype(BF)
    chosen = chosen.astype(BF)
    feat = tokens.shape[2]
    sent[:, :feat] = dot(chosen, tokens[0], ((1,), (0,))).astype(BF)
    sent[:, feat:] = dot(chosen, out_grad[0], ((1,), (0,))).astype(BF)


def dispatch(base, picks, tokens, out_grad, slots):
    exp_count, pick_total = picks.shape[1:]
    tok_dev, feat = tokens.shape[1:]
    lows = 16
    steps = 2
    rows = exp_count * slots // steps

    def whole(shape):
        return pl.BlockSpec(shape, lambda i: (0,) * len(shape))

    return pl.pallas_call(
        dispatch_kernel,
        grid=(steps,),
        in_specs=[
            pl.BlockSpec(memory_space=pltpu.SMEM),
            whole(picks.shape),
            whole(tokens.shape),
            whole(out_grad.shape),
        ],
        out_specs=[
            pl.BlockSpec((rows, 2 * feat), lambda i: (i, 0)),
            pl.BlockSpec((tok_dev, rows), lambda i: (0, i)),
        ],
        out_shape=[
            jax.ShapeDtypeStruct((exp_count * slots, 2 * feat), BF),
            jax.ShapeDtypeStruct((tok_dev, exp_count * slots), BF),
        ],
        scratch_shapes=[
            pltpu.VMEM((exp_count * tok_dev // lows, pick_total), F32),
            pltpu.VMEM((exp_count * lows, pick_total), F32),
            pltpu.VMEM((exp_count, tok_dev), F32),
        ],
        compiler_params=pltpu.CompilerParams(vmem_limit_bytes=60 * 1024 * 1024),
        cost_estimate=pl.CostEstimate(
            flops=4 * exp_count * slots * tok_dev * feat,
            bytes_accessed=4 * exp_count * slots * feat,
            transcendentals=0,
        ),
    )(jnp.reshape(base, (1,)).astype(I32), picks, tokens, out_grad)


def expert_kernel(scale, core, gate, in_hbm, out_hbm, rows, gate_slot, *refs):
    outs, refs = refs[:5], refs[5:]
    weight_in, in_turned, weight_out, out_turned, held = refs[:5]
    grads, out_theirs, in_theirs, out_mine, in_mine, pre, gated, in_sems, out_sems = refs[5:]
    count, feat = grads.shape
    hid = pre.shape[1]
    chunks = 1
    size = count // chunks
    copy_of = pltpu.make_async_copy

    def chunk(i, part):
        at = (pl.ds(i * size, size), pl.ds(part * feat, feat))
        return copy_of(rows.at[at], held.at[at], in_sems.at[2 * i + part])

    loads = [
        copy_of(out_hbm, weight_out, in_sems.at[2 * chunks]),
        copy_of(in_hbm, weight_in, in_sems.at[2 * chunks + 1]),
    ]
    loads += [chunk(i, part) for i in range(chunks) for part in range(2)]
    for load in loads:
        load.start()
    sent = []

    def send(source, target):
        sent.append(copy_of(source, target, out_sems.at[len(sent)]))
        sent[-1].start()

    lanes = 128
    wide = jnp.broadcast_to(gate[...], (lanes, count)).T
    wide = jnp.concatenate([wide] * (hid // lanes), axis=1)
    loads[0].wait()
    out_turned[...] = weight_out[...].T
    loads[1].wait()
    in_turned[...] = weight_in[...].T
    for i in range(chunks):
        at = slice(i * size, (i + 1) * size)
        loads[2 + 2 * i].wait()
        pre_act = dot(held[at, :feat], weight_in[...], ((1,), (0,)))
        loads[3 + 2 * i].wait()
        back = dot(held[at, feat:], out_turned[...], ((1,), (0,)))
        sig = 1.0 / (1.0 + jnp.exp(-pre_act))
        activation = (pre_act * sig).astype(BF).astype(F32)
        terms = activation * back
        terms = sum(terms[:, k : k + lanes] for k in range(0, hid, lanes))
        gate_slot[:, at] = jnp.sum(terms.T, axis=0, keepdims=True)
        gated[at, :] = (wide[at, :] * activation).astype(BF)
        pre_grad = (wide[at, :] * back * (sig * (1.0 + pre_act * (1.0 - sig)))).astype(BF)
        pre[at, :] = pre_grad
        grads[at, :] = dot(pre_grad, in_turned[...], ((1,), (0,))).astype(BF)
        place = pl.ds(i * size, size)
        send(grads.at[place, :], outs[0].at[place, :])

    def theirs_first(ref):
        low, high = ref[:, : hid // 2], ref[:, hid // 2 :]
        first = core[0] == 0
        return jnp.concatenate((jnp.where(first, high, low), jnp.where(first, low, high)), axis=1)

    gated_pair, pre_pair = theirs_first(gated), theirs_first(pre)
    width = 512
    for first in range(0, feat, width):
        at = slice(first, first + width)
        grad_at = slice(feat + first, feat + first + width)
        out = (dot(gated_pair, held[:, grad_at], ((0,), (0,))) * scale).astype(BF)
        out_theirs[:, at], out_mine[:, at] = out[: hid // 2], out[hid // 2 :]
        inn = (dot(held[:, at], pre_pair, ((0,), (0,))) * scale).astype(BF)
        in_theirs[at, :], in_mine[at, :] = inn[:, : hid // 2], inn[:, hid // 2 :]
        place = pl.ds(first, width)
        send(out_theirs.at[:, place], outs[1].at[:, place])
        send(in_theirs.at[place, :], outs[2].at[place, :])
        send(out_mine.at[:, place], outs[3].at[:, place])
        send(in_mine.at[place, :], outs[4].at[place, :])
    for copy in sent:
        copy.wait()


def expert_pass(rows, weight_in, weight_out, gate, core, scale):
    count, feat, hid = rows.shape[0], weight_in.shape[0], weight_in.shape[1]
    vmem = pl.BlockSpec(memory_space=pltpu.VMEM)
    anywhere = pl.BlockSpec(memory_space=pl.ANY)
    shapes = [(count, feat)] + [(hid // 2, feat), (feat, hid // 2)] * 2
    held = [(feat, hid), (hid, feat), (hid, feat), (feat, hid), rows.shape]
    held += shapes + [(count, hid)] * 2
    gate_slot, grads, *parts = pl.pallas_call(
        functools.partial(expert_kernel, scale),
        in_specs=[pl.BlockSpec(memory_space=pltpu.SMEM), vmem] + [anywhere] * 3,
        out_specs=[vmem] + [anywhere] * 5,
        out_shape=[jax.ShapeDtypeStruct((1, count), F32)]
        + [jax.ShapeDtypeStruct(shape, BF) for shape in shapes],
        scratch_shapes=[pltpu.VMEM(shape, BF) for shape in held]
        + [pltpu.SemaphoreType.DMA((4,)), pltpu.SemaphoreType.DMA((17,))],
        compiler_params=pltpu.CompilerParams(vmem_limit_bytes=58 * 1024 * 1024),
        cost_estimate=pl.CostEstimate(
            flops=10 * count * feat * hid,
            bytes_accessed=4 * (count * feat + feat * hid),
            transcendentals=count * hid,
        ),
    )(jnp.reshape(core, (1,)).astype(I32), gate, weight_in, weight_out, rows)
    return grads, gate_slot, parts[:2], parts[2:]


def assemble_kernel(where, *refs):
    out_pieces, in_pieces = refs[:8], refs[8:16]
    out_ref, in_ref, sems = refs[16:]
    core, near, far = where[0], where[1], where[2]
    out_rows, in_rows, in_cols = out_pieces[0].shape[0], in_pieces[0].shape[0], in_pieces[0].shape[1]
    copies = []
    for k in range(8):
        half = core if k < 4 else 1 - core
        flip_b, flip_a = k % 2, (k // 2) % 2
        a = 1 - near if flip_a else near
        b = 1 - far if flip_b else far
        row = pl.multiple_of(((half * 2 + a) * 2 + b) * out_rows, out_rows)
        place = out_ref.at[pl.ds(row, out_rows), :]
        copies.append(pltpu.make_async_copy(out_pieces[k], place, sems.at[2 * k]))
        a = 1 - far if flip_a else far
        b = 1 - near if flip_b else near
        row = pl.multiple_of((a * 2 + b) * in_rows, in_rows)
        col = pl.multiple_of(half * in_cols, in_cols)
        place = in_ref.at[pl.ds(row, in_rows), pl.ds(col, in_cols)]
        copies.append(pltpu.make_async_copy(in_pieces[k], place, sems.at[2 * k + 1]))
    for copy in copies:
        copy.start()
    for copy in copies:
        copy.wait()


def assemble(where, out_pieces, in_pieces, out_shape, in_shape):
    moved = 4 * (out_shape[0] * out_shape[1] + in_shape[0] * in_shape[1])
    return pl.pallas_call(
        assemble_kernel,
        in_specs=[pl.BlockSpec(memory_space=pltpu.SMEM)]
        + [pl.BlockSpec(memory_space=pltpu.VMEM)] * 16,
        out_specs=[pl.BlockSpec(memory_space=pl.ANY)] * 2,
        out_shape=[jax.ShapeDtypeStruct(out_shape, BF), jax.ShapeDtypeStruct(in_shape, BF)],
        scratch_shapes=[pltpu.SemaphoreType.DMA((16,))],
        compiler_params=pltpu.CompilerParams(vmem_limit_bytes=24 * 1024 * 1024),
        cost_estimate=pl.CostEstimate(flops=0, bytes_accessed=moved, transcendentals=0),
    )(where, *out_pieces, *in_pieces)


def shards(tokens, out_grad, w_in, w_out, picks, gates):
    ctx_count = lax.axis_size("ctx")
    exp_count = lax.axis_size("expert")
    core = lax.axis_index("dp")
    ctx_index = lax.axis_index("ctx")
    exp_index = lax.axis_index("expert")
    tok_dev, feat = tokens.shape[1], tokens.shape[2]
    hid = w_in.shape[2]
    pick_total = picks.shape[2]
    share = pick_total // ctx_count
    slots = ctx_count * 4
    grad_scale = (lax.axis_size("dp") * pick_total) ** (-0.5)
    lists = picks[0]
    before = earlier(tok_dev)
    tok_ids = jnp.arange(tok_dev, dtype=I32)

    def swap(rows):
        out = rows.reshape(exp_count, -1, rows.shape[1])
        out = lax.all_to_all(out, "expert", split_axis=0, concat_axis=0, tiled=True)
        return out.reshape(rows.shape)

    base = (ctx_index * exp_count + exp_index) * tok_dev
    sent, spread = dispatch(base, picks, tokens, out_grad, slots)
    arrived = swap(sent)

    own = lax.dynamic_index_in_dim(lists, exp_index, 0, keepdims=False)
    offset = own - ctx_index * (exp_count * tok_dev)
    block = offset // tok_dev
    inside = (block >= 0) & (block < exp_count)
    token = offset % tok_dev
    in_block = (inside[:, None] & (block[:, None] == jnp.arange(exp_count)[None, :])).astype(BF)
    at_token = (token[:, None] == tok_ids[None, :]).astype(BF)
    held = dot(in_block, at_token, ((0,), (0,))).astype(BF)
    rank_own = dot(held, before, ((1,), (0,))).astype(BF)
    rank_pick = jnp.sum(
        dot(in_block, rank_own, ((1,), (0,))) * at_token.astype(F32), axis=1
    ).astype(I32)
    gate_mine = gates[0, 0]
    gate_all = jnp.zeros((ctx_count, share), F32)
    gate_all = lax.dynamic_update_slice_in_dim(gate_all, gate_mine[None], ctx_index, 0)
    for step in range(1, ctx_count):
        got = lax.ppermute(gate_mine, "ctx", ring(ctx_count, step))
        gate_all = lax.dynamic_update_slice_in_dim(
            gate_all, got[None], (ctx_index - step) % ctx_count, 0
        )
    gate_all = gate_all.reshape(pick_total)

    place = jnp.where(inside, block * slots + rank_pick, -1)
    at_slot = place[:, None] == jnp.arange(exp_count * slots, dtype=I32)[None, :]
    slot_gate = jnp.sum(jnp.where(at_slot, gate_all[:, None], 0.0), axis=0)[None, :]

    row_grads, gate_slot, theirs, mine = expert_pass(
        arrived, w_in[0], w_out[0], slot_gate, core, grad_scale
    )
    got = [lax.ppermute(part, "dp", SWAP) for part in theirs]
    row_grads, _ = lax.optimization_barrier((row_grads, theirs))
    returned = swap(row_grads)
    halves = [(a.astype(F32) + b.astype(F32)).astype(BF) for a, b in zip(mine, got)]

    gate_pick = jnp.sum(jnp.where(at_slot, gate_slot, 0.0), axis=1)
    gate_rows = gate_pick.reshape(ctx_count, share)
    gate_grad = lax.dynamic_index_in_dim(gate_rows, ctx_index, 0, keepdims=False)
    for step in range(1, ctx_count):
        term = lax.dynamic_index_in_dim(
            gate_rows, (ctx_index + step) % ctx_count, 0, keepdims=False
        )
        gate_grad = gate_grad + lax.ppermute(term, "ctx", ring(ctx_count, step))

    near, far = bits(ctx_index)
    pieces, gate_grad = reduce_ctx(halves, near, far, gate_grad)
    token_total = dot(spread, returned, ((1,), (0,))).astype(BF)
    pieces = [four + tuple(lax.ppermute(term, "dp", SWAP) for term in four) for four in pieces]
    pieces, token_total = lax.optimization_barrier((pieces, token_total))
    out_total, in_total = assemble(
        jnp.stack((core, near, far)).astype(I32), *pieces, (hid, feat), (feat, hid)
    )

    return (
        token_total[None],
        in_total[None],
        out_total[None],
        gate_grad.reshape(1, 1, share),
    )


def solution(mesh):
    placed = (
        P("dp", ("ctx", "expert"), None),
        P("dp", ("ctx", "expert"), None),
        P("expert", None, None),
        P("expert", None, None),
        P("dp", None, None),
        P("dp", "expert", "ctx"),
    )
    return jax.shard_map(
        shards,
        mesh=mesh,
        in_specs=placed,
        out_specs=(
            P("dp", ("ctx", "expert"), None),
            P("expert", None, None),
            P("expert", None, None),
            P("dp", "expert", "ctx"),
        ),
        check_vma=False,
    )
```
